256 devices in a mesh: section: 4 (over x), dp: 16 (over y, z_lo, core), tensor: 4 (over z_hi).
Axes of the slice: x: 4, y: 4, z: 8 (z_hi: 4, z_lo: 2; z = z_hi * 2 + z_lo), core: 2. Of those that a mesh axis runs over, the one named last changes fastest.
Arguments:
- inputs: bfloat16 [4, 1024, 1024], P(None, ('dp', 'tensor')), may hold values from -16 to 16
- gains: float32 [4, 1024], P('section'), may hold values from 0.1 to 1.9
- w_up: bfloat16 [4, 1024, 4096], P('section', None, 'tensor'), may hold values from -0.1875 to 0.1875
- w_down: bfloat16 [4, 4096, 1024], P('section', 'tensor'), may hold values from -0.09375 to 0.09375
- out_grad: bfloat16 [4, 1024, 1024], P(None, ('dp', 'tensor')), may hold values from -0.5 to 0.5
Outputs:
- up_grads: float32 [4, 1024, 4096], P('section', 'dp', 'tensor')
- down_grads: float32 [4, 4096, 1024], P('section', 'tensor', 'dp')
- gain_grads: float32 [4, 1024], P('section', ('dp', 'tensor'))
The draws below stay inside these ranges and needn't reach their ends.
All inputs are finite; a program needn't handle non-finite values.
Results may differ from the reference program's by a relative error of at most 0.035.
Values may be sent and summed in bfloat16 or wider, within the bound.
A program may use at most 64 MiB of HBM per device.

```python
import math
import jax
import jax.numpy as jnp
from jax import lax

D = 1024
HID_DEV = 1024
MICRO = 4
TOK_MB = 64
HID = 4096
TOKENS = 1024
LAYERS = 4
N_SECTION = 4
N_DP = 16
N_TENSOR = 4


def raised(entries, rng, source, target, blocks, factor):
    def block_of(axis_at):
        return (jnp.arange(entries.shape[axis_at]) // (entries.shape[axis_at] // blocks)).reshape((-1,) + (1,) * (entries.ndim - 1 - axis_at))

    near = jax.random.permutation(rng, blocks)[block_of(target)]
    far = (block_of(target) + blocks // 2) % blocks
    return jnp.where((block_of(source) == near) | (block_of(source) == far), factor * entries, entries)


def block_scale(own_key, shape, cuts, smallest, high):
    factor_of = 1.0
    for dim, parts in cuts:
        draws = jax.random.uniform(jax.random.fold_in(jax.random.fold_in(own_key, 6), dim), (parts,), jnp.float32, smallest / len(cuts), high / len(cuts))
        factor_of = factor_of * jnp.repeat(jnp.exp(draws), shape[dim] // parts).reshape((-1,) + (1,) * (len(shape) - 1 - dim))
    return factor_of


def gaussian(key, extent, scale, limit, shards=(), dtype=jnp.bfloat16):
    gain = block_scale(key, extent, shards, -0.22, 0.18) if shards else 1.0
    entries = jax.random.normal(key, extent, jnp.float32) * scale * gain
    return jnp.minimum(jnp.maximum(entries, -limit), limit).astype(dtype)


def heavy_noise(own_key, dims, width, bound, split, heavy, dtype=jnp.bfloat16):
    array = width * jax.random.normal(own_key, dims, jnp.float32)
    if split:
        array = array * block_scale(own_key, dims, split, -0.22, 0.18)
    return jnp.clip(raised(array, jax.random.fold_in(own_key, 3), *heavy), -bound, bound).astype(dtype)


def setup_inputs(seed: int = 0) -> dict:
    keys = jax.random.split(jax.random.key(seed), 6)
    inputs = heavy_noise(keys[0], (MICRO, TOKENS, D), 1.0, 16.0, ((1, 64),), (1, 2, 64, 4.0))
    gains = jnp.clip(1.0 + 0.18 * jax.random.normal(keys[1], (LAYERS, D), jnp.float32), 0.1, 1.9)
    w_up = gaussian(keys[2], (LAYERS, D, HID), D ** -0.5, 0.1875, ((0, 4), (2, 4)))
    w_down = gaussian(keys[3], (LAYERS, HID, D), HID ** -0.5, 0.09375, ((0, 4), (1, 4)))
    out_grad = heavy_noise(keys[4], (MICRO, TOKENS, D), 0.03, 0.5, ((1, 64),), (1, 2, 64, 4.0))
    return dict(inputs=inputs, gains=gains, w_up=w_up, w_down=w_down, out_grad=out_grad)


norm_eps = 1e-05
gelu_coef = 0.044715

def normalize(hidden):
    values = hidden.astype(jnp.float32)
    centre = values - lax.optimization_barrier(jnp.mean(values, axis=-1, keepdims=True))
    spread = lax.optimization_barrier(jnp.mean(centre * centre, axis=-1, keepdims=True))
    scale = lax.rsqrt(spread + norm_eps)
    return (centre * scale, scale)

def gelu_slope(preact):
    root = math.sqrt(2.0 / math.pi)
    inner = root * (preact + gelu_coef * preact * preact * preact)
    tangent = jnp.tanh(inner)
    return 0.5 * (1.0 + tangent) + 0.5 * preact * (1.0 - tangent * tangent) * root * (1.0 + 3.0 * gelu_coef * preact * preact)

def norm_back(upstream, normed, scale, gain_row):
    scaled = upstream * gain_row
    return scale * (scaled - lax.optimization_barrier(jnp.mean(scaled, axis=-1, keepdims=True)) - normed * lax.optimization_barrier(jnp.mean(scaled * normed, axis=-1, keepdims=True)))

def down_project(activated, weight):
    total = jnp.zeros((activated.shape[0], weight.shape[1]), jnp.float32)
    for group in range(N_TENSOR):
        start = group * HID_DEV
        part = jnp.dot(activated[:, start:start + HID_DEV], weight[start:start + HID_DEV], preferred_element_type=jnp.float32)
        total = total + lax.optimization_barrier(part.astype(jnp.bfloat16)).astype(jnp.float32)
    return total

def up_project(preact_grad, weight):
    total = jnp.zeros((preact_grad.shape[0], weight.shape[0]), jnp.float32)
    for group in range(N_TENSOR):
        start = group * HID_DEV
        part = lax.dot_general(preact_grad[:, start:start + HID_DEV], weight[:, start:start + HID_DEV], (((1,), (1,)), ((), ())), preferred_element_type=jnp.float32)
        total = total + lax.optimization_barrier(part.astype(jnp.bfloat16)).astype(jnp.float32)
    return total

def replica_sum(left, right):
    left_cols = left.shape[-1]
    right_cols = right.shape[-1]
    left_split = left.reshape(MICRO, N_DP, TOK_MB, left_cols)
    right_split = right.reshape(MICRO, N_DP, TOK_MB, right_cols)
    total = jnp.zeros((left_cols, right_cols), jnp.float32)
    for replica in range(N_DP):
        part = lax.dot_general(left_split[:, replica].reshape(-1, left_cols), right_split[:, replica].reshape(-1, right_cols), (((0,), (0,)), ((), ())), preferred_element_type=jnp.float32)
        total = total + lax.optimization_barrier(part.astype(jnp.bfloat16)).astype(jnp.float32)
    return total

def reference(inputs, gains, w_up, w_down, out_grad):
    total_rows = MICRO * TOKENS
    hidden = inputs.reshape(total_rows, D)
    saved = []
    for layer in range(N_SECTION):
        normed, scale = normalize(hidden)
        norm_rows = (normed * gains[layer]).astype(jnp.bfloat16)
        preact = jnp.dot(norm_rows, w_up[layer], preferred_element_type=jnp.float32)
        activated = jax.nn.gelu(preact, approximate=True).astype(jnp.bfloat16)
        saved.append((hidden, norm_rows, preact, activated))
        if layer + 1 < N_SECTION:
            hidden = (hidden.astype(jnp.float32) + down_project(activated, w_down[layer])).astype(jnp.bfloat16)
    gradient = out_grad.reshape(total_rows, D)
    up_list = [None] * N_SECTION
    down_list = [None] * N_SECTION
    gain_list = [None] * N_SECTION
    for layer in reversed(range(N_SECTION)):
        hidden, norm_rows, preact, activated = saved[layer]
        normed, scale = normalize(hidden)
        down_grad = lax.dot_general(gradient, w_down[layer], (((1,), (1,)), ((), ())), preferred_element_type=jnp.float32)
        preact_grad = (down_grad * gelu_slope(preact)).astype(jnp.bfloat16)
        norm_grad = up_project(preact_grad, w_up[layer])
        gain_list[layer] = lax.optimization_barrier(jnp.sum(norm_grad * normed, axis=0))
        up_list[layer] = replica_sum(norm_rows, preact_grad)
        down_list[layer] = replica_sum(activated, gradient)
        gradient = (gradient.astype(jnp.float32) + norm_back(norm_grad, normed, scale, gains[layer])).astype(jnp.bfloat16)
    return (jnp.stack(up_list), jnp.stack(down_list), jnp.stack(gain_list))
```

```python
import functools
import math

import jax
import jax.numpy as jnp
from jax import lax
from jax.experimental import pallas as pl
from jax.experimental.pallas import tpu as pltpu
from jax.sharding import PartitionSpec as P

MESH = pl.DeviceIdType.MESH
BF16 = jnp.bfloat16
F32 = jnp.float32
EPS = 1e-05
COEF = 0.044715
ROOT = math.sqrt(2.0 / math.pi)
RING = 8


def dot(left, right, dims):
    return lax.dot_general(left, right, ((dims[:1], dims[1:]), ((), ())), preferred_element_type=F32)


def stats(rows):
    centre = rows - jnp.mean(rows, axis=-1, keepdims=True)
    spread = jnp.mean(centre * centre, axis=-1, keepdims=True)
    scale = lax.rsqrt(spread + EPS)
    return centre * scale, scale


def kernel(
    inp, gains, wu_h, wd_h, og,
    up_o, dn_o, gain_o,
    wu, wd, h_full, part_f, send_f, g_full, part_b, send_b,
    normed_s, scale_s, norm_s, slope_s, act_all, pg_all, nc_all, gc_all,
    up_acc, dn_acc, up_send, dn_send, up_in, dn_in,
    gain_acc, g1, g2,
    loc, agf_s, agf_r, rsf_s, rsf_r, agb_s, agb_r, rsb_s, rsb_r,
    act_ss, act_r, nc_ss, nc_r, pg_ss, pg_r, gc_ss, gc_r,
    up_ss, up_r, dn_ss, dn_r, g1_ss, g1_r, g2_ss, g2_r,
    *, sections, n_y,
):
    micro, rows, width = inp.shape
    full = 4 * rows
    span = width // n_y
    share = span // 4
    s = lax.axis_index("section")
    p = lax.axis_index("dp")
    t = lax.axis_index("tensor")
    core = p % 2
    z_lo = (p // 2) % 2
    y = p // 4
    z = 2 * t + z_lo
    e = 2 * z_lo - 1

    def place(section, y_at, z_at, core_at):
        z_at = (z_at + 2 * RING) % RING
        return (section, (y_at * 2 + z_at % 2) * 2 + core_at, z_at // 2)

    def send(src, dst, ssem, rsem, device):
        pltpu.make_async_remote_copy(
            src_ref=src, dst_ref=dst, send_sem=ssem, recv_sem=rsem,
            device_id=device, device_id_type=MESH,
        ).start()

    def wait(region, sem):
        pltpu.make_async_copy(region, region, sem).wait()

    load_wu = pltpu.make_async_copy(wu_h.at[0], wu, loc.at[0])
    load_wd = pltpu.make_async_copy(wd_h.at[0], wd, loc.at[1])
    first = s == 0
    last = s == sections - 1

    @pl.when(first)
    def _():
        pltpu.make_async_copy(inp, h_full.at[:, pl.ds(0, rows)], loc.at[2]).start()

    @pl.when(last)
    def _():
        pltpu.make_async_copy(og, g_full.at[:, pl.ds(0, rows)], loc.at[3]).start()

    load_wu.start()
    load_wd.start()

    barrier = pltpu.get_barrier_semaphore()

    def greet(device):
        pl.semaphore_signal(barrier, inc=1, device_id=device, device_id_type=MESH)

    for dz in range(RING):
        for dc in range(2):
            if dz or dc:
                greet(place(s, y, z + dz, (core + dc) % 2))
    for dy in range(1, n_y):
        greet(place(s, (y + dy) % n_y, z, core))
    for step in (-2, 0, 1, 2, 3):
        @pl.when(jnp.logical_not(first))
        def _():
            greet(place(s - 1, y, z + e * step, core))

        @pl.when(jnp.logical_not(last))
        def _():
            greet(place(s + 1, y, z + e * step, core))

    within = 2 * RING - 1 + n_y - 1
    edge = jnp.logical_or(first, last)

    @pl.when(edge)
    def _():
        pl.semaphore_wait(barrier, within + 5 * (sections > 1))

    @pl.when(jnp.logical_not(edge))
    def _():
        pl.semaphore_wait(barrier, within + 10)

    peers = ((1, 1), (2, -2), (3, 3))

    def gather(buf, m, ssem, rsem):
        for slot, step in peers:
            send(
                buf.at[m, pl.ds(0, rows)], buf.at[m, pl.ds(slot * rows, rows)],
                ssem.at[m], rsem.at[m], place(s, y, z + e * step, core),
            )

    def scatter(src, dst, m, ssem, rsem, section):
        for slot in range(4):
            send(
                src.at[m, pl.ds(slot * rows, rows)], dst.at[m, slot],
                ssem.at[m], rsem.at[m], place(section, y, z + e * slot, core),
            )

    def to_y(buf, m, ssem, rsem):
        for dy in range(1, n_y):
            send(buf.at[m, 0], buf.at[m, dy], ssem.at[m], rsem.at[m], place(s, (y + dy) % n_y, z, core))

    def cols_to_y(src, buf, m, ssem, rsem):
        for dy in range(1, n_y):
            y_at = (y + dy) % n_y
            send(
                src.at[m, :, pl.ds(pl.multiple_of(y_at * span, span), span)], buf.at[m, dy],
                ssem.at[m], rsem.at[m], place(s, y_at, z, core),
            )

    own_cols = pl.ds(pl.multiple_of(y * span, span), span)
    gain_row = gains[...]

    def rows_f(m):
        @pl.when(jnp.logical_not(first))
        def _():
            wait(part_f.at[m], rsf_r.at[m])
            total = part_f[m, 0].astype(F32)
            for slot in range(1, 4):
                total = total + part_f[m, slot].astype(F32)
            h_full[m, pl.ds(0, rows)] = total.astype(BF16)

        gather(h_full, m, agf_s, agf_r)

    def step_f(m):
        wait(h_full.at[m, pl.ds(rows, 3 * rows)], agf_r.at[m])
        hidden = h_full[m].astype(F32)
        normed, scale = stats(hidden)
        norm = (normed * gain_row).astype(BF16)
        preact = dot(norm, wu[...], (1, 0))
        inner = ROOT * (preact + COEF * preact * preact * preact)
        tangent = jnp.tanh(inner)
        act = (0.5 * preact * (1.0 + tangent)).astype(BF16)
        act_all[m, 0] = act

        @pl.when(jnp.logical_not(last))
        def _():
            mixed = dot(act, wd[...], (1, 0))
            send_f[m, pl.ds(0, rows)] = (mixed[:rows] + hidden[:rows]).astype(BF16)
            send_f[m, pl.ds(rows, 3 * rows)] = mixed[rows:].astype(BF16)
            scatter(send_f, part_f, m, rsf_s, rsf_r, s + 1)

        slope_s[m] = 0.5 * (1.0 + tangent) + 0.5 * preact * (1.0 - tangent * tangent) * ROOT * (
            1.0 + 3.0 * COEF * preact * preact
        )
        normed_s[m] = normed
        scale_s[m] = jnp.broadcast_to(scale, (full, 128))
        norm_s[m] = norm
        nc_all[m, 0] = norm_s[m, :, own_cols]
        cols_to_y(norm_s, nc_all, m, nc_ss, nc_r)
        to_y(act_all, m, act_ss, act_r)

    @pl.when(first)
    def _():
        pltpu.make_async_copy(inp, h_full.at[:, pl.ds(0, rows)], loc.at[2]).wait()

    rows_f(0)

    @pl.when(last)
    def _():
        pltpu.make_async_copy(og, g_full.at[:, pl.ds(0, rows)], loc.at[3]).wait()
        for m in range(micro):
            gather(g_full, m, agb_s, agb_r)

    load_wu.wait()
    load_wd.wait()

    def loop_f(m, carry):
        @pl.when(m < micro - 1)
        def _():
            rows_f(m + 1)

        step_f(m)
        return carry

    lax.fori_loop(0, micro, loop_f, 0)

    gain_acc[...] = jnp.zeros_like(gain_acc)

    def rows_b(m):
        @pl.when(jnp.logical_not(last))
        def _():
            wait(part_b.at[m], rsb_r.at[m])
            total = part_b[m, 0].astype(F32)
            for slot in range(1, 4):
                total = total + part_b[m, slot].astype(F32)
            g_full[m, pl.ds(0, rows)] = total.astype(BF16)
            gather(g_full, m, agb_s, agb_r)

    def step_b(m):
        wait(g_full.at[m, pl.ds(rows, 3 * rows)], agb_r.at[m])
        grad = g_full[m]
        down_grad = dot(grad, wd[...], (1, 1))
        pg = (down_grad * slope_s[m]).astype(BF16)
        pg_all[m, 0] = pg
        to_y(pg_all, m, pg_ss, pg_r)
        norm_grad = dot(pg, wu[...], (1, 1))
        normed = normed_s[m]

        @pl.when(jnp.logical_not(first))
        def _():
            scaled = norm_grad * gain_row
            back = scale_s[m][:, :1] * (
                scaled
                - jnp.mean(scaled, axis=-1, keepdims=True)
                - normed * jnp.mean(scaled * normed, axis=-1, keepdims=True)
            )
            send_b[m, pl.ds(0, rows)] = (back[:rows] + grad[:rows].astype(F32)).astype(BF16)
            send_b[m, pl.ds(rows, 3 * rows)] = back[rows:].astype(BF16)
            scatter(send_b, part_b, m, rsb_s, rsb_r, s - 1)

        terms = norm_grad * normed
        total = terms[0:8]
        for at in range(8, full, 8):
            total = total + terms[at:at + 8]
        gain_acc[...] += total
        gc_all[m, 0] = g_full[m, :, own_cols]
        cols_to_y(g_full, gc_all, m, gc_ss, gc_r)

    rows_b(0)

    def loop_b(m, carry):
        @pl.when(m < micro - 1)
        def _():
            rows_b(m + 1)

        step_b(m)
        return carry

    lax.fori_loop(0, micro, loop_b, 0)

    total = jnp.sum(gain_acc[...], axis=0, keepdims=True)
    lines = width // 128
    for line in range(lines):
        g1[0, line:line + 1] = total[:, line * 128:(line + 1) * 128]
    for dy in range(1, n_y):
        send(g1.at[0], g1.at[dy], g1_ss.at[0], g1_r.at[0], place(s, (y + dy) % n_y, z, core))

    dn_acc[...] = jnp.zeros_like(dn_acc)
    up_acc[...] = jnp.zeros_like(up_acc)

    def down_part(m, carry):
        if n_y > 1:
            wait(act_all.at[m, pl.ds(1, n_y - 1)], act_r.at[m])
            wait(gc_all.at[m, pl.ds(1, n_y - 1)], gc_r.at[m])
        cols = gc_all[m].reshape(n_y * full, span)
        dn_acc[...] += dot(cols, act_all[m].reshape(n_y * full, -1), (0, 0))
        return carry

    def up_part(m, carry):
        if n_y > 1:
            wait(nc_all.at[m, pl.ds(1, n_y - 1)], nc_r.at[m])
            wait(pg_all.at[m, pl.ds(1, n_y - 1)], pg_r.at[m])
        cols = nc_all[m].reshape(n_y * full, span)
        up_acc[...] += dot(cols, pg_all[m].reshape(n_y * full, -1), (0, 0))
        return carry

    def exchange(acc, out, into, ssem, rsem):
        out[...] = acc[...].astype(BF16)
        for rel in range(1, 4):
            z_lo_at = (z_lo + rel // 2) % 2
            core_at = (core + rel % 2) % 2
            block = z_lo_at * 2 + core_at
            send(
                out.at[pl.ds(pl.multiple_of(block * share, share), share)], into.at[rel - 1],
                ssem.at[0], rsem.at[0], place(s, y, 2 * t + z_lo_at, core_at),
            )

    own_block = pl.ds(pl.multiple_of((z_lo * 2 + core) * share, share), share)

    def finish(acc, into):
        total = acc[own_block]
        for rel in range(3):
            total = total + into[rel].astype(F32)
        return total

    lax.fori_loop(0, micro - 1, up_part, 0)
    lax.fori_loop(0, micro, down_part, 0)
    exchange(dn_acc, dn_send, dn_in, dn_ss, dn_r)
    up_part(micro - 1, 0)
    exchange(up_acc, up_send, up_in, up_ss, up_r)

    if n_y > 1:
        wait(g1.at[pl.ds(1, n_y - 1)], g1_r.at[0])
    total = g1[0]
    for dy in range(1, n_y):
        total = total + g1[dy]
    g2[0] = total
    for dz in range(RING):
        for dc in range(2):
            if dz or dc:
                send(
                    g2.at[0], g2.at[dz * 2 + dc], g2_ss.at[0], g2_r.at[0],
                    place(s, y, z + dz, (core + dc) % 2),
                )

    wait(dn_in, dn_r.at[0])
    dn_o[0] = finish(dn_acc, dn_in).T

    wait(g2.at[pl.ds(1, 2 * RING - 1)], g2_r.at[0])
    total = g2[0]
    for peer in range(1, 2 * RING):
        total = total + g2[peer]
    per = gain_o.shape[1]
    fold = 128 // per
    index = p * 4 + t
    line_at = lax.broadcasted_iota(jnp.int32, total.shape, 0)
    line = jnp.sum(jnp.where(line_at == index // fold, total, 0.0), axis=0, keepdims=True)
    piece = jnp.zeros((1, per), F32)
    for at in range(fold):
        piece = piece + jnp.where(index % fold == at, line[:, at * per:(at + 1) * per], 0.0)
    gain_o[...] = piece

    wait(up_in, up_r.at[0])
    up_o[0] = finish(up_acc, up_in)

    def drain(m, carry):
        wait(h_full.at[m, pl.ds(rows, 3 * rows)], agf_s.at[m])
        wait(g_full.at[m, pl.ds(rows, 3 * rows)], agb_s.at[m])

        @pl.when(jnp.logical_not(last))
        def _():
            wait(part_f.at[m], rsf_s.at[m])

        @pl.when(jnp.logical_not(first))
        def _():
            wait(part_b.at[m], rsb_s.at[m])

        if n_y > 1:
            wait(act_all.at[m, pl.ds(1, n_y - 1)], act_ss.at[m])
            wait(pg_all.at[m, pl.ds(1, n_y - 1)], pg_ss.at[m])
            wait(nc_all.at[m, pl.ds(1, n_y - 1)], nc_ss.at[m])
            wait(gc_all.at[m, pl.ds(1, n_y - 1)], gc_ss.at[m])
        return carry

    lax.fori_loop(0, micro, drain, 0)
    if n_y > 1:
        wait(g1.at[pl.ds(1, n_y - 1)], g1_ss.at[0])
    wait(g2.at[pl.ds(1, 2 * RING - 1)], g2_ss.at[0])
    wait(dn_in, dn_ss.at[0])
    wait(up_in, up_ss.at[0])


def solution(mesh):
    sections, n_dp, n_tensor = (mesh.shape[axis] for axis in ("section", "dp", "tensor"))
    n_y = n_dp // 4

    def per_device(inputs, gains, w_up, w_down, out_grad):
        micro, rows, width = inputs.shape
        hid = w_up.shape[2]
        full = 4 * rows
        span = width // n_y
        share = span // 4
        per = width // (n_dp * n_tensor)
        any_space = pl.BlockSpec(memory_space=pl.ANY)
        vmem = pl.BlockSpec(memory_space=pltpu.VMEM)
        dma = pltpu.SemaphoreType.DMA
        many, one = dma((micro,)), dma((1,))
        return pl.pallas_call(
            functools.partial(kernel, sections=sections, n_y=n_y),
            out_shape=(
                jax.ShapeDtypeStruct((1, share, hid), F32),
                jax.ShapeDtypeStruct((1, hid, share), F32),
                jax.ShapeDtypeStruct((1, per), F32),
            ),
            in_specs=[any_space, vmem, any_space, any_space, any_space],
            out_specs=(vmem, vmem, vmem),
            scratch_shapes=[
                pltpu.VMEM((width, hid), BF16),
                pltpu.VMEM((hid, width), BF16),
                pltpu.VMEM((micro, full, width), BF16),
                pltpu.VMEM((micro, 4, rows, width), BF16),
                pltpu.VMEM((micro, full, width), BF16),
                pltpu.VMEM((micro, full, width), BF16),
                pltpu.VMEM((micro, 4, rows, width), BF16),
                pltpu.VMEM((micro, full, width), BF16),
                pltpu.VMEM((micro, full, width), F32),
                pltpu.VMEM((micro, full, 128), F32),
                pltpu.VMEM((micro, full, width), BF16),
                pltpu.VMEM((micro, full, hid), F32),
                pltpu.VMEM((micro, n_y, full, hid), BF16),
                pltpu.VMEM((micro, n_y, full, hid), BF16),
                pltpu.VMEM((micro, n_y, full, span), BF16),
                pltpu.VMEM((micro, n_y, full, span), BF16),
                pltpu.VMEM((span, hid), F32),
                pltpu.VMEM((span, hid), F32),
                pltpu.VMEM((span, hid), BF16),
                pltpu.VMEM((span, hid), BF16),
                pltpu.VMEM((3, share, hid), BF16),
                pltpu.VMEM((3, share, hid), BF16),
                pltpu.VMEM((8, width), F32),
                pltpu.VMEM((n_y, width // 128, 128), F32),
                pltpu.VMEM((2 * RING, width // 128, 128), F32),
                dma((4,)),
            ] + [many] * 16 + [one] * 8,
            compiler_params=pltpu.CompilerParams(
                collective_id=0, has_side_effects=True, vmem_limit_bytes=50 * 1024 * 1024
            ),
        )(inputs, gains, w_up, w_down, out_grad)

    return jax.shard_map(
        per_device,
        mesh=mesh,
        in_specs=(
            P(None, ("dp", "tensor"), None),
            P("section", None),
            P("section", None, "tensor"),
            P("section", "tensor", None),
            P(None, ("dp", "tensor"), None),
        ),
        out_specs=(
            P("section", "dp", "tensor"),
            P("section", "tensor", "dp"),
            P("section", ("dp", "tensor")),
        ),
        check_vma=False,
    )
```

```python
import functools
import math

import jax
import jax.numpy as jnp
from jax import lax
from jax.experimental import pallas as pl
from jax.experimental.pallas import tpu as pltpu
from jax.sharding import PartitionSpec as P

MESH = pl.DeviceIdType.MESH
BF16 = jnp.bfloat16
F32 = jnp.float32
EPS = 1e-05
COEF = 0.044715
ROOT = math.sqrt(2.0 / math.pi)
RING = 8


def dot(left, right, dims):
    return lax.dot_general(left, right, ((dims[:1], dims[1:]), ((), ())), preferred_element_type=F32)


def stats(rows):
    centre = rows - jnp.mean(rows, axis=-1, keepdims=True)
    spread = jnp.mean(centre * centre, axis=-1, keepdims=True)
    scale = lax.rsqrt(spread + EPS)
    return centre * scale, scale


def kernel(
    inp, gains_h, wu_h, wd_h, og,
    up_o, dn_o, gain_o,
    wu, wd, h_full, part_f, send_f, g_full, part_b, send_b,
    gains, normed_s, scale_s, norm_s, slope_s, act_all, pg_all, nc_all, gc_all,
    wu_t, wd_t, up_acc, dn_acc, up_buf, dn_buf,
    gain_acc, g1, g2,
    loc, agf_s, agf_r, rsf_s, rsf_r, agb_s, agb_r, rsb_s, rsb_r,
    act_ss, act_r, nc_ss, nc_r, pg_ss, pg_r, gc_ss, gc_r,
    up_ss, up_r, dn_ss, dn_r, up2_ss, up2_r, dn2_ss, dn2_r, g1_ss, g1_r, g2_ss, g2_r,
    *, sections, n_y,
):
    micro, rows, width = inp.shape
    full = 4 * rows
    span = width // n_y
    share = span // 4
    s = lax.axis_index("section")
    p = lax.axis_index("dp")
    t = lax.axis_index("tensor")
    core = p % 2
    z_lo = (p // 2) % 2
    y = p // 4
    z = 2 * t + z_lo
    e = 2 * z_lo - 1

    def place(section, y_at, z_at, core_at):
        z_at = (z_at + 2 * RING) % RING
        return (section, (y_at * 2 + z_at % 2) * 2 + core_at, z_at // 2)

    def send(src, dst, ssem, rsem, device):
        pltpu.make_async_remote_copy(
            src_ref=src, dst_ref=dst, send_sem=ssem, recv_sem=rsem,
            device_id=device, device_id_type=MESH,
        ).start()

    def wait(region, sem):
        pltpu.make_async_copy(region, region, sem).wait()

    load_wu = pltpu.make_async_copy(wu_h.at[0], wu, loc.at[0])
    load_wd = pltpu.make_async_copy(wd_h.at[0], wd, loc.at[1])
    first = s == 0
    last = s == sections - 1

    @pl.when(first)
    def _():
        pltpu.make_async_copy(inp, h_full.at[:, pl.ds(0, rows)], loc.at[2]).start()

    @pl.when(last)
    def _():
        pltpu.make_async_copy(og, g_full.at[:, pl.ds(0, rows)], loc.at[3]).start()

    load_gains = pltpu.make_async_copy(gains_h, gains, loc.at[4])
    load_gains.start()
    load_wu.start()
    load_wd.start()

    barrier = pltpu.get_barrier_semaphore()

    def greet(device):
        pl.semaphore_signal(barrier, inc=1, device_id=device, device_id_type=MESH)

    for dz in range(RING):
        for dc in range(2):
            if dz or dc:
                greet(place(s, y, z + dz, (core + dc) % 2))
    for dy in range(1, n_y):
        greet(place(s, (y + dy) % n_y, z, core))
    for step in (-2, 0, 1, 2, 3):
        @pl.when(jnp.logical_not(first))
        def _():
            greet(place(s - 1, y, z + e * step, core))

        @pl.when(jnp.logical_not(last))
        def _():
            greet(place(s + 1, y, z + e * step, core))

    within = 2 * RING - 1 + n_y - 1
    edge = jnp.logical_or(first, last)

    @pl.when(edge)
    def _():
        pl.semaphore_wait(barrier, within + 5 * (sections > 1))

    @pl.when(jnp.logical_not(edge))
    def _():
        pl.semaphore_wait(barrier, within + 10)

    peers = ((3, 3), (2, -2), (1, 1))

    def gather(buf, m, ssem, rsem):
        for slot, step in peers:
            send(
                buf.at[m, pl.ds(0, rows)], buf.at[m, pl.ds(slot * rows, rows)],
                ssem.at[m], rsem.at[m], place(s, y, z + e * step, core),
            )

    def scatter(src, dst, m, ssem, rsem, section):
        for slot in (3, 2, 1, 0):
            send(
                src.at[m, pl.ds(slot * rows, rows)], dst.at[m, slot],
                ssem.at[m], rsem.at[m], place(section, y, z + e * slot, core),
            )

    def to_y(buf, m, ssem, rsem):
        for dy in range(1, n_y):
            send(buf.at[m, 0], buf.at[m, dy], ssem.at[m], rsem.at[m], place(s, (y + dy) % n_y, z, core))

    def cols_to_y(src, buf, m, ssem, rsem):
        for dy in range(1, n_y):
            y_at = (y + dy) % n_y
            send(
                src.at[m, :, pl.ds(pl.multiple_of(y_at * span, span), span)], buf.at[m, dy],
                ssem.at[m], rsem.at[m], place(s, y_at, z, core),
            )

    own_cols = pl.ds(pl.multiple_of(y * span, span), span)

    def rows_f(m):
        @pl.when(jnp.logical_not(first))
        def _():
            wait(part_f.at[m], rsf_r.at[m])
            total = part_f[m, 0].astype(F32)
            for slot in range(1, 4):
                total = total + part_f[m, slot].astype(F32)
            h_full[m, pl.ds(0, rows)] = total.astype(BF16)

        gather(h_full, m, agf_s, agf_r)

    def step_f(m):
        wait(h_full.at[m, pl.ds(rows, 3 * rows)], agf_r.at[m])
        hidden = h_full[m].astype(F32)
        normed, scale = stats(hidden)
        norm = (normed * gain_row).astype(BF16)
        preact = dot(norm, wu[...], (1, 0))
        inner = ROOT * (preact + COEF * preact * preact * preact)
        tangent = jnp.tanh(inner)
        act = (0.5 * preact * (1.0 + tangent)).astype(BF16)
        act_all[m, 0] = act

        @pl.when(jnp.logical_not(last))
        def _():
            mixed = dot(act, wd[...], (1, 0))
            send_f[m, pl.ds(0, rows)] = (mixed[:rows] + hidden[:rows]).astype(BF16)
            send_f[m, pl.ds(rows, 3 * rows)] = mixed[rows:].astype(BF16)
            scatter(send_f, part_f, m, rsf_s, rsf_r, s + 1)

        slope_s[m] = 0.5 * (1.0 + tangent) + 0.5 * preact * (1.0 - tangent * tangent) * ROOT * (
            1.0 + 3.0 * COEF * preact * preact
        )
        normed_s[m] = normed
        scale_s[m] = jnp.broadcast_to(scale, (full, 128))
        norm_s[m] = norm
        nc_all[m, 0] = norm_s[m, :, own_cols]
        cols_to_y(norm_s, nc_all, m, nc_ss, nc_r)
        to_y(act_all, m, act_ss, act_r)

    @pl.when(first)
    def _():
        pltpu.make_async_copy(inp, h_full.at[:, pl.ds(0, rows)], loc.at[2]).wait()

    @pl.when(jnp.logical_not(last))
    def _():
        rows_f(0)

    @pl.when(last)
    def _():
        pltpu.make_async_copy(og, g_full.at[:, pl.ds(0, rows)], loc.at[3]).wait()
        for m in range(micro):
            gather(g_full, m, agb_s, agb_r)

    load_gains.wait()
    load_wu.wait()
    load_wd.wait()
    gain_row = gains[...]

    gain_acc[...] = jnp.zeros_like(gain_acc)

    def rows_b(m):
        @pl.when(jnp.logical_not(last))
        def _():
            wait(part_b.at[m], rsb_r.at[m])
            total = part_b[m, 0].astype(F32)
            for slot in range(1, 4):
                total = total + part_b[m, slot].astype(F32)
            g_full[m, pl.ds(0, rows)] = total.astype(BF16)
            gather(g_full, m, agb_s, agb_r)

    def step_b(m):
        wait(g_full.at[m, pl.ds(rows, 3 * rows)], agb_r.at[m])
        grad = g_full[m]
        down_grad = dot(grad, wd_t[...], (1, 0))
        pg = (down_grad * slope_s[m]).astype(BF16)
        pg_all[m, 0] = pg
        to_y(pg_all, m, pg_ss, pg_r)
        gc_all[m, 0] = g_full[m, :, own_cols]
        cols_to_y(g_full, gc_all, m, gc_ss, gc_r)
        norm_grad = dot(pg, wu_t[...], (1, 0))
        normed = normed_s[m]

        @pl.when(jnp.logical_not(first))
        def _():
            scaled = norm_grad * gain_row
            back = scale_s[m][:, :1] * (
                scaled
                - jnp.mean(scaled, axis=-1, keepdims=True)
                - normed * jnp.mean(scaled * normed, axis=-1, keepdims=True)
            )
            send_b[m, pl.ds(0, rows)] = (back[:rows] + grad[:rows].astype(F32)).astype(BF16)
            send_b[m, pl.ds(rows, 3 * rows)] = back[rows:].astype(BF16)
            scatter(send_b, part_b, m, rsb_s, rsb_r, s - 1)

        terms = norm_grad * normed
        total = terms[0:8]
        for at in range(8, full, 8):
            total = total + terms[at:at + 8]
        gain_acc[...] += total

    def transpose(weight, into):
        step = 256
        count = weight.shape[0] // step

        def piece(at, carry):
            part = pl.ds(pl.multiple_of(at * step, step), step)
            into[:, part] = weight[part].T
            return carry

        lax.fori_loop(0, count, piece, 0)

    @pl.when(jnp.logical_not(first))
    def _():
        transpose(wd, wd_t)
        transpose(wu, wu_t)

    turn = s // (sections - 1)

    def step(i, carry):
        back = turn * (i % 2) + (1 - turn) * (i // micro)
        m = turn * (i // 2) + (1 - turn) * (i % micro)
        ahead = m + 1 - turn

        @pl.when(back == 0)
        def _():
            @pl.when(ahead < micro)
            def _():
                rows_f(ahead)

            step_f(m)

        @pl.when(back == 1)
        def _():
            @pl.when(jnp.logical_and(first, m == 0))
            def _():
                transpose(wd, wd_t)
                transpose(wu, wu_t)

            rows_b(m)
            step_b(m)

        return carry

    lax.fori_loop(0, 2 * micro, step, 0)

    total = jnp.sum(gain_acc[...], axis=0, keepdims=True)
    lines = width // 128
    for line in range(lines):
        g1[0, line:line + 1] = total[:, line * 128:(line + 1) * 128]
    for dy in range(1, n_y):
        send(g1.at[0], g1.at[dy], g1_ss.at[0], g1_r.at[0], place(s, (y + dy) % n_y, z, core))

    dn_acc[...] = jnp.zeros_like(dn_acc)
    up_acc[...] = jnp.zeros_like(up_acc)

    def down_part(m, carry):
        if n_y > 1:
            wait(act_all.at[m, pl.ds(1, n_y - 1)], act_r.at[m])
            wait(gc_all.at[m, pl.ds(1, n_y - 1)], gc_r.at[m])
        cols = gc_all[m].reshape(n_y * full, span)
        dn_acc[...] += dot(cols, act_all[m].reshape(n_y * full, -1), (0, 0))
        return carry

    def up_part(m, carry):
        if n_y > 1:
            wait(nc_all.at[m, pl.ds(1, n_y - 1)], nc_r.at[m])
            wait(pg_all.at[m, pl.ds(1, n_y - 1)], pg_r.at[m])
        cols = nc_all[m].reshape(n_y * full, span)
        up_acc[...] += dot(cols, pg_all[m].reshape(n_y * full, -1), (0, 0))
        return carry

    other = 1 - core

    def block(z_lo_at, core_at):
        return pl.ds(pl.multiple_of((z_lo_at * 2 + core_at) * share, share), share)

    def to_core(acc, buf, ssem, rsem):
        for z_lo_at in range(2):
            buf[z_lo_at] = acc[block(z_lo_at, other)].astype(BF16)
        send(buf.at[pl.ds(0, 2)], buf.at[pl.ds(2, 2)], ssem.at[0], rsem.at[0], place(s, y, z, other))

    def to_pair(acc, buf, rsem, ssem2, rsem2):
        wait(buf.at[pl.ds(2, 2)], rsem.at[0])
        away = 1 - z_lo
        buf[4] = (acc[block(away, core)] + buf[2 + away].astype(F32)).astype(BF16)
        send(buf.at[4], buf.at[5], ssem2.at[0], rsem2.at[0], place(s, y, 2 * t + away, core))

    def finish(acc, buf, rsem2):
        wait(buf.at[5], rsem2.at[0])
        return acc[block(z_lo, core)] + buf[2 + z_lo].astype(F32) + buf[5].astype(F32)

    lax.fori_loop(0, micro - 1, up_part, 0)
    lax.fori_loop(0, micro, down_part, 0)
    to_core(dn_acc, dn_buf, dn_ss, dn_r)

    if n_y > 1:
        wait(g1.at[pl.ds(1, n_y - 1)], g1_r.at[0])
    total = g1[0]
    for dy in range(1, n_y):
        total = total + g1[dy]
    g2[0] = total
    for dz in range(RING):
        for dc in range(2):
            if dz or dc:
                send(
                    g2.at[0], g2.at[dz * 2 + dc], g2_ss.at[0], g2_r.at[0],
                    place(s, y, z + dz, (core + dc) % 2),
                )

    to_pair(dn_acc, dn_buf, dn_r, dn2_ss, dn2_r)
    up_part(micro - 1, 0)
    to_core(up_acc, up_buf, up_ss, up_r)
    to_pair(up_acc, up_buf, up_r, up2_ss, up2_r)
    dn_o[0] = finish(dn_acc, dn_buf, dn2_r)

    wait(g2.at[pl.ds(1, 2 * RING - 1)], g2_r.at[0])
    total = g2[0]
    for peer in range(1, 2 * RING):
        total = total + g2[peer]
    per = gain_o.shape[1]
    fold = 128 // per
    index = p * 4 + t
    line_at = lax.broadcasted_iota(jnp.int32, total.shape, 0)
    line = jnp.sum(jnp.where(line_at == index // fold, total, 0.0), axis=0, keepdims=True)
    piece = jnp.zeros((1, per), F32)
    for at in range(fold):
        piece = piece + jnp.where(index % fold == at, line[:, at * per:(at + 1) * per], 0.0)
    gain_o[...] = piece

    up_o[0] = finish(up_acc, up_buf, up2_r)

    def drain(m, carry):
        wait(h_full.at[m, pl.ds(rows, 3 * rows)], agf_s.at[m])
        wait(g_full.at[m, pl.ds(rows, 3 * rows)], agb_s.at[m])

        @pl.when(jnp.logical_not(last))
        def _():
            wait(part_f.at[m], rsf_s.at[m])

        @pl.when(jnp.logical_not(first))
        def _():
            wait(part_b.at[m], rsb_s.at[m])

        if n_y > 1:
            wait(act_all.at[m, pl.ds(1, n_y - 1)], act_ss.at[m])
            wait(pg_all.at[m, pl.ds(1, n_y - 1)], pg_ss.at[m])
            wait(nc_all.at[m, pl.ds(1, n_y - 1)], nc_ss.at[m])
            wait(gc_all.at[m, pl.ds(1, n_y - 1)], gc_ss.at[m])
        return carry

    lax.fori_loop(0, micro, drain, 0)
    if n_y > 1:
        wait(g1.at[pl.ds(1, n_y - 1)], g1_ss.at[0])
    wait(g2.at[pl.ds(1, 2 * RING - 1)], g2_ss.at[0])
    wait(dn_buf.at[pl.ds(0, 2)], dn_ss.at[0])
    wait(up_buf.at[pl.ds(0, 2)], up_ss.at[0])
    wait(dn_buf.at[4], dn2_ss.at[0])
    wait(up_buf.at[4], up2_ss.at[0])


def solution(mesh):
    sections, n_dp, n_tensor = (mesh.shape[axis] for axis in ("section", "dp", "tensor"))
    n_y = n_dp // 4

    def per_device(inputs, gains, w_up, w_down, out_grad):
        micro, rows, width = inputs.shape
        hid = w_up.shape[2]
        full = 4 * rows
        span = width // n_y
        share = span // 4
        per = width // (n_dp * n_tensor)
        hbm = pl.BlockSpec(memory_space=pltpu.HBM)
        vmem = pl.BlockSpec(memory_space=pltpu.VMEM)
        dma = pltpu.SemaphoreType.DMA
        many, one = dma((micro,)), dma((1,))
        up, down, gain = pl.pallas_call(
            functools.partial(kernel, sections=sections, n_y=n_y),
            out_shape=(
                jax.ShapeDtypeStruct((1, share, hid), F32),
                jax.ShapeDtypeStruct((1, share, hid), F32),
                jax.ShapeDtypeStruct((1, per), F32),
            ),
            in_specs=[hbm] * 5,
            out_specs=(vmem, vmem, vmem),
            scratch_shapes=[
                pltpu.VMEM((width, hid), BF16),
                pltpu.VMEM((hid, width), BF16),
                pltpu.VMEM((micro, full, width), BF16),
                pltpu.VMEM((micro, 4, rows, width), BF16),
                pltpu.VMEM((micro, full, width), BF16),
                pltpu.VMEM((micro, full, width), BF16),
                pltpu.VMEM((micro, 4, rows, width), BF16),
                pltpu.VMEM((micro, full, width), BF16),
                pltpu.VMEM((1, width), F32),
                pltpu.VMEM((micro, full, width), F32),
                pltpu.VMEM((micro, full, 128), F32),
                pltpu.VMEM((micro, full, width), BF16),
                pltpu.VMEM((micro, full, hid), F32),
                pltpu.VMEM((micro, n_y, full, hid), BF16),
                pltpu.VMEM((micro, n_y, full, hid), BF16),
                pltpu.VMEM((micro, n_y, full, span), BF16),
                pltpu.VMEM((micro, n_y, full, span), BF16),
                pltpu.VMEM((hid, width), BF16),
                pltpu.VMEM((width, hid), BF16),
                pltpu.VMEM((span, hid), F32),
                pltpu.VMEM((span, hid), F32),
                pltpu.VMEM((6, share, hid), BF16),
                pltpu.VMEM((6, share, hid), BF16),
                pltpu.VMEM((8, width), F32),
                pltpu.VMEM((n_y, width // 128, 128), F32),
                pltpu.VMEM((2 * RING, width // 128, 128), F32),
                dma((5,)),
            ] + [many] * 16 + [one] * 12,
            compiler_params=pltpu.CompilerParams(
                collective_id=0, has_side_effects=True, vmem_limit_bytes=63 * 1024 * 1024
            ),
        )(inputs, gains, w_up, w_down, out_grad)
        return up, jnp.swapaxes(down, 1, 2), gain

    return jax.shard_map(
        per_device,
        mesh=mesh,
        in_specs=(
            P(None, ("dp", "tensor"), None),
            P("section", None),
            P("section", None, "tensor"),
            P("section", "tensor", None),
            P(None, ("dp", "tensor"), None),
        ),
        out_specs=(
            P("section", "dp", "tensor"),
            P("section", "tensor", "dp"),
            P("section", ("dp", "tensor")),
        ),
        check_vma=False,
    )
```

```python
import functools
import math

import jax
import jax.numpy as jnp
from jax import lax
from jax.experimental import pallas as pl
from jax.experimental.pallas import tpu as pltpu
from jax.sharding import PartitionSpec as P

MESH = pl.DeviceIdType.MESH
BF16 = jnp.bfloat16
F32 = jnp.float32
EPS = 1e-05
COEF = 0.044715
ROOT = math.sqrt(2.0 / math.pi)
RING = 8


def dot(left, right, dims):
    return lax.dot_general(left, right, ((dims[:1], dims[1:]), ((), ())), preferred_element_type=F32)


def stats(rows):
    centre = rows - jnp.mean(rows, axis=-1, keepdims=True)
    spread = jnp.mean(centre * centre, axis=-1, keepdims=True)
    scale = lax.rsqrt(spread + EPS)
    return centre * scale, scale


def kernel(
    inp, gains_h, wu_h, wd_h, og,
    up_o, dn_o, gain_o,
    wu, wd, own, h_full, part_f, sum_f, send_f, g_full, part_b, sum_b, send_b,
    gains, normed_s, scale_s, norm_s, slope_s, act_all, pg_all, nc_all, gc_all,
    wu_t, wd_t, up_acc, dn_acc, up_buf, dn_buf,
    gain_acc, g1, g2,
    loc, own_s, agf_s, agf_r, rsf_s, rsf_r, agb_s, agb_r, rsb_s, rsb_r,
    act_ss, act_r, nc_ss, nc_r, pg_ss, pg_r, gc_ss, gc_r,
    up_ss, up_r, dn_ss, dn_r, up2_ss, up2_r, dn2_ss, dn2_r, g1_ss, g1_r, g2_ss, g2_r,
    *, sections, n_y,
):
    micro, rows, width = inp.shape
    full = 4 * rows
    span = width // n_y
    share = span // 4
    s = lax.axis_index("section")
    p = lax.axis_index("dp")
    t = lax.axis_index("tensor")
    core = p % 2
    z_lo = (p // 2) % 2
    y = p // 4
    z = 2 * t + z_lo
    e = 2 * z_lo - 1

    def place(section, y_at, z_at, core_at):
        z_at = (z_at + 2 * RING) % RING
        return (section, (y_at * 2 + z_at % 2) * 2 + core_at, z_at // 2)

    def send(src, dst, ssem, rsem, device):
        pltpu.make_async_remote_copy(
            src_ref=src, dst_ref=dst, send_sem=ssem, recv_sem=rsem,
            device_id=device, device_id_type=MESH,
        ).start()

    def wait(region, sem):
        pltpu.make_async_copy(region, region, sem).wait()

    load_wu = pltpu.make_async_copy(wu_h.at[0], wu, loc.at[0])
    load_wd = pltpu.make_async_copy(wd_h.at[0], wd, loc.at[1])
    first = s == 0
    last = s == sections - 1

    load_in = pltpu.make_async_copy(inp.at[s], own.at[0], loc.at[2])
    load_og = pltpu.make_async_copy(og.at[s], own.at[1], loc.at[3])
    load_in.start()
    load_og.start()
    load_gains = pltpu.make_async_copy(gains_h, gains, loc.at[4])
    load_gains.start()
    load_wu.start()
    load_wd.start()

    barrier = pltpu.get_barrier_semaphore()

    def greet(device):
        pl.semaphore_signal(barrier, inc=1, device_id=device, device_id_type=MESH)

    for dz in range(RING):
        for dc in range(2):
            if dz or dc:
                greet(place(s, y, z + dz, (core + dc) % 2))
    for dy in range(1, n_y):
        greet(place(s, (y + dy) % n_y, z, core))
    for ds in range(1, sections):
        for step in (-2, 0, 1, 2, 3):
            greet(place((s + ds) % sections, y, z + e * step, core))
    pl.semaphore_wait(barrier, 2 * RING - 1 + n_y - 1 + 5 * (sections - 1))

    def gather(src, dst, ssem, rsem, section, slots=((3, 3), (2, -2), (1, 1), (0, 0))):
        for slot, step in slots:
            send(src, dst.at[pl.ds(slot * rows, rows)], ssem, rsem, place(section, y, z + e * step, core))

    def scatter(src, dst, ssem, rsem, section):
        for slot in (3, 2, 1, 0):
            send(src.at[pl.ds(slot * rows, rows)], dst.at[slot], ssem, rsem, place(section, y, z + e * slot, core))

    def relay(part, total_ref, part_r, ssem, dst, rsem, section):
        wait(part, part_r)
        total = part[0].astype(F32)
        for slot in range(1, 4):
            total = total + part[slot].astype(F32)
        total_ref[...] = total.astype(BF16)
        gather(total_ref, dst, ssem, rsem, section)

    def relay_f(duty, m, section):
        at = duty * micro + m
        relay(part_f.at[at], sum_f.at[at], rsf_r.at[at], agf_s.at[at], h_full.at[m], agf_r.at[m], section)

    def relay_b(m, section):
        relay(part_b.at[m], sum_b.at[m], rsb_r.at[m], agb_s.at[m], g_full.at[m], agb_r.at[m], section)

    ring_y = sorted(range(1, n_y), key=lambda dy: -min(dy, n_y - dy))

    def to_y(buf, m, ssem, rsem):
        for dy in ring_y:
            send(buf.at[m, 0], buf.at[m, dy], ssem.at[m], rsem.at[m], place(s, (y + dy) % n_y, z, core))

    def cols_to_y(src, buf, m, ssem, rsem):
        for dy in ring_y:
            y_at = (y + dy) % n_y
            send(
                src.at[m, :, pl.ds(pl.multiple_of(y_at * span, span), span)], buf.at[m, dy],
                ssem.at[m], rsem.at[m], place(s, y_at, z, core),
            )

    own_cols = pl.ds(pl.multiple_of(y * span, span), span)

    def step_f(m):
        wait(h_full.at[m], agf_r.at[m])
        hidden = h_full[m].astype(F32)
        normed, scale = stats(hidden)
        norm = (normed * gain_row).astype(BF16)
        preact = dot(norm, wu[...], (1, 0))
        inner = ROOT * (preact + COEF * preact * preact * preact)
        tangent = jnp.tanh(inner)
        act = (0.5 * preact * (1.0 + tangent)).astype(BF16)
        act_all[m, 0] = act

        @pl.when(jnp.logical_not(last))
        def _():
            mixed = dot(act, wd[...], (1, 0))
            send_f[m, pl.ds(0, rows)] = (mixed[:rows] + hidden[:rows]).astype(BF16)
            send_f[m, pl.ds(rows, 3 * rows)] = mixed[rows:].astype(BF16)
            at = s // 2 * micro + m

            @pl.when(m > 0)
            def _():
                wait(h_full.at[m - 1], rsf_s.at[m - 1])

            scatter(send_f.at[m], part_f.at[at], rsf_s.at[m], rsf_r.at[at], (s + 3) % 4 - s // 2)

        slope_s[m] = 0.5 * (1.0 + tangent) + 0.5 * preact * (1.0 - tangent * tangent) * ROOT * (
            1.0 + 3.0 * COEF * preact * preact
        )
        normed_s[m] = normed
        scale_s[m] = jnp.broadcast_to(scale, (full, 128))
        norm_s[m] = norm
        nc_all[m, 0] = norm_s[m, :, own_cols]
        cols_to_y(norm_s, nc_all, m, nc_ss, nc_r)
        to_y(act_all, m, act_ss, act_r)

    load_in.wait()
    far = ((3, 3), (2, -2), (1, 1))

    def spread(which, dst, rsem, section):
        gather(own.at[which], dst.at[s], own_s.at[which], rsem.at[s], section, far)

        @pl.when(s == section)
        def _():
            pltpu.make_async_copy(own.at[which], dst.at[s, pl.ds(0, rows)], rsem.at[s]).start()

        @pl.when(s != section)
        def _():
            gather(own.at[which], dst.at[s], own_s.at[which], rsem.at[s], section, ((0, 0),))

    spread(0, h_full, agf_r, 0)
    load_og.wait()
    spread(1, g_full, agb_r, sections - 1)
    load_gains.wait()
    load_wu.wait()
    load_wd.wait()
    gain_row = gains[...]

    gain_acc[...] = jnp.zeros_like(gain_acc)

    def step_b(m):
        wait(g_full.at[m], agb_r.at[m])
        grad = g_full[m]
        down_grad = dot(grad, wd_t[...], (1, 0))
        pg = (down_grad * slope_s[m]).astype(BF16)
        pg_all[m, 0] = pg
        to_y(pg_all, m, pg_ss, pg_r)
        gc_all[m, 0] = g_full[m, :, own_cols]
        cols_to_y(g_full, gc_all, m, gc_ss, gc_r)
        norm_grad = dot(pg, wu_t[...], (1, 0))
        normed = normed_s[m]

        @pl.when(jnp.logical_not(first))
        def _():
            scaled = norm_grad * gain_row
            back = scale_s[m][:, :1] * (
                scaled
                - jnp.mean(scaled, axis=-1, keepdims=True)
                - normed * jnp.mean(scaled * normed, axis=-1, keepdims=True)
            )
            send_b[m, pl.ds(0, rows)] = (back[:rows] + grad[:rows].astype(F32)).astype(BF16)
            send_b[m, pl.ds(rows, 3 * rows)] = back[rows:].astype(BF16)
            scatter(send_b.at[m], part_b.at[m], rsb_s.at[m], rsb_r.at[m], (s + 1) % 4 + s // 3)

        terms = norm_grad * normed
        total = terms[0:8]
        for at in range(8, full, 8):
            total = total + terms[at:at + 8]
        gain_acc[...] += total

    def transpose(weight, into):
        step = 256
        count = weight.shape[0] // step

        def piece(at, carry):
            part = pl.ds(pl.multiple_of(at * step, step), step)
            into[:, part] = weight[part].T
            return carry

        lax.fori_loop(0, count, piece, 0)

    @pl.when(jnp.logical_not(first))
    def _():
        transpose(wd, wd_t)
        transpose(wu, wu_t)

    def helping(start, stop, body):
        def run(m, carry):
            body(m)
            return carry

        lax.fori_loop(start, stop, run, 0)

    @pl.when(last)
    def _():
        helping(0, micro, lambda m: relay_f(0, m, 1))

    turn = s // (sections - 1)

    def step(i, carry):
        back = turn * (i % 2) + (1 - turn) * (i // micro)
        m = turn * (i // 2) + (1 - turn) * (i % micro)

        @pl.when(back == 0)
        def _():
            step_f(m)

        @pl.when(back == 1)
        def _():
            @pl.when(jnp.logical_and(first, m == 0))
            def _():
                helping(0, micro, lambda m: relay_f(0, m, 2))
                helping(0, micro, lambda m: relay_f(1, m, 3))
                transpose(wd, wd_t)
                transpose(wu, wu_t)

            @pl.when(jnp.logical_and(s == 1, m == 0))
            def _():
                helping(0, micro, lambda m: relay_b(m, 2))

            step_b(m)

        return carry

    lax.fori_loop(0, 2 * micro, step, 0)

    @pl.when(s >= 2)
    def _():
        helping(0, micro, lambda m: relay_b(m, s - 2))

    total = jnp.sum(gain_acc[...], axis=0, keepdims=True)
    lines = width // 128
    for line in range(lines):
        g1[0, line:line + 1] = total[:, line * 128:(line + 1) * 128]
    for dy in range(1, n_y):
        send(g1.at[0], g1.at[dy], g1_ss.at[0], g1_r.at[0], place(s, (y + dy) % n_y, z, core))

    dn_acc[...] = jnp.zeros_like(dn_acc)
    up_acc[...] = jnp.zeros_like(up_acc)

    def down_part(m, carry):
        if n_y > 1:
            wait(act_all.at[m, pl.ds(1, n_y - 1)], act_r.at[m])
            wait(gc_all.at[m, pl.ds(1, n_y - 1)], gc_r.at[m])
        cols = gc_all[m].reshape(n_y * full, span)
        dn_acc[...] += dot(cols, act_all[m].reshape(n_y * full, -1), (0, 0))
        return carry

    def up_part(m, carry):
        if n_y > 1:
            wait(nc_all.at[m, pl.ds(1, n_y - 1)], nc_r.at[m])
            wait(pg_all.at[m, pl.ds(1, n_y - 1)], pg_r.at[m])
        cols = nc_all[m].reshape(n_y * full, span)
        up_acc[...] += dot(cols, pg_all[m].reshape(n_y * full, -1), (0, 0))
        return carry

    other = 1 - core

    def block(z_lo_at, core_at):
        return pl.ds(pl.multiple_of((z_lo_at * 2 + core_at) * share, share), share)

    def to_core(acc, buf, ssem, rsem):
        for z_lo_at in range(2):
            buf[z_lo_at] = acc[block(z_lo_at, other)].astype(BF16)
        send(buf.at[pl.ds(0, 2)], buf.at[pl.ds(2, 2)], ssem.at[0], rsem.at[0], place(s, y, z, other))

    def to_pair(acc, buf, rsem, ssem2, rsem2):
        wait(buf.at[pl.ds(2, 2)], rsem.at[0])
        away = 1 - z_lo
        buf[4] = (acc[block(away, core)] + buf[2 + away].astype(F32)).astype(BF16)
        send(buf.at[4], buf.at[5], ssem2.at[0], rsem2.at[0], place(s, y, 2 * t + away, core))

    def finish(acc, buf, rsem2):
        wait(buf.at[5], rsem2.at[0])
        return acc[block(z_lo, core)] + buf[2 + z_lo].astype(F32) + buf[5].astype(F32)

    lax.fori_loop(0, micro - 1, up_part, 0)
    lax.fori_loop(0, micro, down_part, 0)
    to_core(dn_acc, dn_buf, dn_ss, dn_r)

    if n_y > 1:
        wait(g1.at[pl.ds(1, n_y - 1)], g1_r.at[0])
    total = g1[0]
    for dy in range(1, n_y):
        total = total + g1[dy]
    g2[0] = total
    for dz in range(RING):
        for dc in range(2):
            if dz or dc:
                send(
                    g2.at[0], g2.at[dz * 2 + dc], g2_ss.at[0], g2_r.at[0],
                    place(s, y, z + dz, (core + dc) % 2),
                )

    to_pair(dn_acc, dn_buf, dn_r, dn2_ss, dn2_r)
    up_part(micro - 1, 0)
    to_core(up_acc, up_buf, up_ss, up_r)
    to_pair(up_acc, up_buf, up_r, up2_ss, up2_r)
    dn_o[0] = finish(dn_acc, dn_buf, dn2_r)

    wait(g2.at[pl.ds(1, 2 * RING - 1)], g2_r.at[0])
    total = g2[0]
    for peer in range(1, 2 * RING):
        total = total + g2[peer]
    per = gain_o.shape[1]
    fold = 128 // per
    index = p * 4 + t
    line_at = lax.broadcasted_iota(jnp.int32, total.shape, 0)
    line = jnp.sum(jnp.where(line_at == index // fold, total, 0.0), axis=0, keepdims=True)
    piece = jnp.zeros((1, per), F32)
    for at in range(fold):
        piece = piece + jnp.where(index % fold == at, line[:, at * per:(at + 1) * per], 0.0)
    gain_o[...] = piece

    up_o[0] = finish(up_acc, up_buf, up2_r)

    def drain(m, carry):
        @pl.when(jnp.logical_or(first, last))
        def _():
            wait(h_full.at[m], agf_s.at[m])

        @pl.when(first)
        def _():
            wait(h_full.at[m], agf_s.at[micro + m])

        @pl.when(jnp.logical_not(last))
        def _():
            @pl.when(m == micro - 1)
            def _():
                wait(h_full.at[m], rsf_s.at[m])

        @pl.when(jnp.logical_not(first))
        def _():
            wait(g_full.at[m], agb_s.at[m])
            wait(g_full.at[m], rsb_s.at[m])

        if n_y > 1:
            wait(act_all.at[m, pl.ds(1, n_y - 1)], act_ss.at[m])
            wait(pg_all.at[m, pl.ds(1, n_y - 1)], pg_ss.at[m])
            wait(nc_all.at[m, pl.ds(1, n_y - 1)], nc_ss.at[m])
            wait(gc_all.at[m, pl.ds(1, n_y - 1)], gc_ss.at[m])
        return carry

    lax.fori_loop(0, micro, drain, 0)
    for which, section in ((0, 0), (1, sections - 1)):
        wait(h_full.at[0, pl.ds(0, 3 * rows)], own_s.at[which])

        @pl.when(s != section)
        def _():
            wait(h_full.at[0, pl.ds(0, rows)], own_s.at[which])

    if n_y > 1:
        wait(g1.at[pl.ds(1, n_y - 1)], g1_ss.at[0])
    wait(g2.at[pl.ds(1, 2 * RING - 1)], g2_ss.at[0])
    wait(dn_buf.at[pl.ds(0, 2)], dn_ss.at[0])
    wait(up_buf.at[pl.ds(0, 2)], up_ss.at[0])
    wait(dn_buf.at[4], dn2_ss.at[0])
    wait(up_buf.at[4], up2_ss.at[0])


def settle(up, down, gain, up_o, down_o, gain_o):
    up_o[...] = up[...]
    down_o[...] = down[...]
    gain_o[...] = gain[...]


def solution(mesh):
    sections, n_dp, n_tensor = (mesh.shape[axis] for axis in ("section", "dp", "tensor"))
    n_y = n_dp // 4

    def per_device(inputs, gains, w_up, w_down, out_grad):
        micro, rows, width = inputs.shape
        hid = w_up.shape[2]
        full = 4 * rows
        span = width // n_y
        share = span // 4
        per = width // (n_dp * n_tensor)
        hbm = pl.BlockSpec(memory_space=pltpu.HBM)
        vmem = pl.BlockSpec(memory_space=pltpu.VMEM)
        dma = pltpu.SemaphoreType.DMA
        many, one = dma((micro,)), dma((1,))
        up, down, gain = pl.pallas_call(
            functools.partial(kernel, sections=sections, n_y=n_y),
            out_shape=(
                jax.ShapeDtypeStruct((1, share, hid), F32),
                jax.ShapeDtypeStruct((1, share, hid), F32),
                jax.ShapeDtypeStruct((1, per), F32),
            ),
            in_specs=[hbm] * 5,
            out_specs=(vmem, vmem, vmem),
            scratch_shapes=[
                pltpu.VMEM((width, hid), BF16),
                pltpu.VMEM((hid, width), BF16),
                pltpu.VMEM((2, rows, width), BF16),
                pltpu.VMEM((micro, full, width), BF16),
                pltpu.VMEM((2 * micro, 4, rows, width), BF16),
                pltpu.VMEM((2 * micro, rows, width), BF16),
                pltpu.VMEM((micro, full, width), BF16),
                pltpu.VMEM((micro, full, width), BF16),
                pltpu.VMEM((micro, 4, rows, width), BF16),
                pltpu.VMEM((micro, rows, width), BF16),
                pltpu.VMEM((micro, full, width), BF16),
                pltpu.VMEM((1, width), F32),
                pltpu.VMEM((micro, full, width), F32),
                pltpu.VMEM((micro, full, 128), F32),
                pltpu.VMEM((micro, full, width), BF16),
                pltpu.VMEM((micro, full, hid), F32),
                pltpu.VMEM((micro, n_y, full, hid), BF16),
                pltpu.VMEM((micro, n_y, full, hid), BF16),
                pltpu.VMEM((micro, n_y, full, span), BF16),
                pltpu.VMEM((micro, n_y, full, span), BF16),
                pltpu.VMEM((hid, width), BF16),
                pltpu.VMEM((width, hid), BF16),
                pltpu.VMEM((span, hid), F32),
                pltpu.VMEM((span, hid), F32),
                pltpu.VMEM((6, share, hid), BF16),
                pltpu.VMEM((6, share, hid), BF16),
                pltpu.VMEM((8, width), F32),
                pltpu.VMEM((n_y, width // 128, 128), F32),
                pltpu.VMEM((2 * RING, width // 128, 128), F32),
                dma((5,)),
                dma((2,)), dma((2 * micro,)), many, many, dma((2 * micro,)),
            ] + [many] * 12 + [one] * 12,
            compiler_params=pltpu.CompilerParams(
                collective_id=0, has_side_effects=True, vmem_limit_bytes=63 * 1024 * 1024
            ),
        )(inputs, gains, w_up, w_down, out_grad)
        up, down, gain = pl.pallas_call(
            settle,
            out_shape=tuple(jax.ShapeDtypeStruct(part.shape, F32) for part in (up, down, gain)),
            in_specs=[vmem] * 3,
            out_specs=(vmem,) * 3,
        )(up, down, gain)
        return up, jnp.swapaxes(down, 1, 2), gain

    return jax.shard_map(
        per_device,
        mesh=mesh,
        in_specs=(
            P(None, ("dp", "tensor"), None),
            P("section", None),
            P("section", None, "tensor"),
            P("section", "tensor", None),
            P(None, ("dp", "tensor"), None),
        ),
        out_specs=(
            P("section", "dp", "tensor"),
            P("section", "tensor", "dp"),
            P("section", ("dp", "tensor")),
        ),
        check_vma=False,
    )
```

```python
import functools
import math

import jax
import jax.numpy as jnp
from jax import lax
from jax.experimental import pallas as pl
from jax.experimental.pallas import tpu as pltpu
from jax.sharding import PartitionSpec as P

MESH = pl.DeviceIdType.MESH
BF16 = jnp.bfloat16
F32 = jnp.float32
EPS = 1e-05
COEF = 0.044715
ROOT = math.sqrt(2.0 / math.pi)
RING = 8


def dot(left, right, dims):
    return lax.dot_general(left, right, ((dims[:1], dims[1:]), ((), ())), preferred_element_type=F32)


def stats(rows):
    centre = rows - jnp.mean(rows, axis=-1, keepdims=True)
    spread = jnp.mean(centre * centre, axis=-1, keepdims=True)
    scale = lax.rsqrt(spread + EPS)
    return centre * scale, scale


def kernel(
    inp, gains_h, wu_h, wd_h, og,
    up_o, dn_o, gain_o,
    wu, wd, own, h_full, part_f, sum_f, send_f, g_full, part_b, sum_b, send_b,
    gains, normed_s, scale_s, norm_s, slope_s, act_all, pg_all, nc_all, gc_all,
    wu_t, wd_t, up_acc, dn_acc, up_buf, dn_buf,
    gain_acc, g1, g2,
    loc, own_s, agf_s, agf_r, rsf_s, rsf_r, agb_s, agb_r, rsb_s, rsb_r,
    act_ss, act_r, nc_ss, nc_r, pg_ss, pg_r, gc_ss, gc_r,
    up_ss, up_r, dn_ss, dn_r, up2_ss, up2_r, dn2_ss, dn2_r, g1_ss, g1_r, g2_ss, g2_r,
    *, sections, n_y,
):
    micro, rows, width = inp.shape
    full = 4 * rows
    span = width // n_y
    share = span // 4
    s = lax.axis_index("section")
    p = lax.axis_index("dp")
    t = lax.axis_index("tensor")
    core = p % 2
    z_lo = (p // 2) % 2
    y = p // 4
    z = 2 * t + z_lo
    e = 2 * z_lo - 1

    def place(section, y_at, z_at, core_at):
        z_at = (z_at + 2 * RING) % RING
        return (section, (y_at * 2 + z_at % 2) * 2 + core_at, z_at // 2)

    def send(src, dst, ssem, rsem, device):
        pltpu.make_async_remote_copy(
            src_ref=src, dst_ref=dst, send_sem=ssem, recv_sem=rsem,
            device_id=device, device_id_type=MESH,
        ).start()

    def wait(region, sem):
        pltpu.make_async_copy(region, region, sem).wait()

    load_wu = pltpu.make_async_copy(wu_h.at[0], wu, loc.at[0])
    load_wd = pltpu.make_async_copy(wd_h.at[0], wd, loc.at[1])
    first = s == 0
    last = s == sections - 1

    load_in = pltpu.make_async_copy(inp.at[s], own.at[0], loc.at[2])
    load_og = pltpu.make_async_copy(og.at[s], own.at[1], loc.at[3])
    load_in.start()
    load_og.start()
    load_gains = pltpu.make_async_copy(gains_h, gains, loc.at[4])
    load_gains.start()
    load_wu.start()
    load_wd.start()

    barrier = pltpu.get_barrier_semaphore()

    def greet(device):
        pl.semaphore_signal(barrier, inc=1, device_id=device, device_id_type=MESH)

    for dz in range(RING):
        for dc in range(2):
            if dz or dc:
                greet(place(s, y, z + dz, (core + dc) % 2))
    for dy in range(1, n_y):
        greet(place(s, (y + dy) % n_y, z, core))
    for ds in range(1, sections):
        for step in (-2, 0, 1, 2, 3):
            greet(place((s + ds) % sections, y, z + e * step, core))
    pl.semaphore_wait(barrier, 2 * RING - 1 + n_y - 1 + 5 * (sections - 1))

    def gather(src, dst, ssem, rsem, section, slots=((3, 3), (2, -2), (1, 1), (0, 0))):
        for slot, step in slots:
            send(src, dst.at[pl.ds(slot * rows, rows)], ssem, rsem, place(section, y, z + e * step, core))

    def scatter(src, dst, ssem, rsem, section):
        for slot in (3, 2, 1, 0):
            send(src.at[pl.ds(slot * rows, rows)], dst.at[slot], ssem, rsem, place(section, y, z + e * slot, core))

    def relay(part, total_ref, part_r, ssem, dst, rsem, section):
        wait(part, part_r)
        total = part[0].astype(F32)
        for slot in range(1, 4):
            total = total + part[slot].astype(F32)
        total_ref[...] = total.astype(BF16)
        gather(total_ref, dst, ssem, rsem, section)

    def relay_f(duty, m, section):
        at = duty * micro + m
        relay(part_f.at[at], sum_f.at[at], rsf_r.at[at], agf_s.at[at], h_full.at[m], agf_r.at[m], section)

    def relay_b(m, section):
        relay(part_b.at[m], sum_b.at[m], rsb_r.at[m], agb_s.at[m], g_full.at[m], agb_r.at[m], section)

    ring_y = sorted(range(1, n_y), key=lambda dy: -min(dy, n_y - dy))

    def to_y(buf, m, ssem, rsem):
        for dy in ring_y:
            send(buf.at[m, 0], buf.at[m, dy], ssem.at[m], rsem.at[m], place(s, (y + dy) % n_y, z, core))

    hid = pg_all.shape[3]
    whole = pl.ds(0, hid)
    halves = (pl.ds(0, hid // 2), pl.ds(hid // 2, hid // 2))

    def pg_to_y(m):
        for half, cols in enumerate(halves):
            for dy in ring_y:
                send(
                    pg_all.at[m, 0, :, cols], pg_all.at[m, dy, :, cols],
                    pg_ss.at[m], pg_r.at[2 * m + half], place(s, (y + dy) % n_y, z, core),
                )

    def cols_to_y(src, buf, m, ssem, rsem):
        for dy in ring_y:
            y_at = (y + dy) % n_y
            send(
                src.at[m, :, pl.ds(pl.multiple_of(y_at * span, span), span)], buf.at[m, dy],
                ssem.at[m], rsem.at[m], place(s, y_at, z, core),
            )

    own_cols = pl.ds(pl.multiple_of(y * span, span), span)

    def step_f(m):
        wait(h_full.at[m], agf_r.at[m])
        hidden = h_full[m].astype(F32)
        normed, scale = stats(hidden)
        norm = (normed * gain_row).astype(BF16)
        preact = dot(norm, wu[...], (1, 0))
        inner = ROOT * (preact + COEF * preact * preact * preact)
        tangent = jnp.tanh(inner)
        act = (0.5 * preact * (1.0 + tangent)).astype(BF16)
        act_all[m, 0] = act

        @pl.when(jnp.logical_not(last))
        def _():
            mixed = dot(act, wd[...], (1, 0))
            send_f[m, pl.ds(0, rows)] = (mixed[:rows] + hidden[:rows]).astype(BF16)
            send_f[m, pl.ds(rows, 3 * rows)] = mixed[rows:].astype(BF16)
            at = s // 2 * micro + m

            @pl.when(m > 0)
            def _():
                wait(h_full.at[m - 1], rsf_s.at[m - 1])

            scatter(send_f.at[m], part_f.at[at], rsf_s.at[m], rsf_r.at[at], (s + 3) % 4)

        slope_s[m] = 0.5 * (1.0 + tangent) + 0.5 * preact * (1.0 - tangent * tangent) * ROOT * (
            1.0 + 3.0 * COEF * preact * preact
        )
        normed_s[m] = normed
        scale_s[m] = jnp.broadcast_to(scale, (full, 128))
        norm_s[m] = norm
        nc_all[m, 0] = norm_s[m, :, own_cols]
        cols_to_y(norm_s, nc_all, m, nc_ss, nc_r)
        to_y(act_all, m, act_ss, act_r)

    load_in.wait()
    far = ((3, 3), (2, -2), (1, 1))

    def spread(which, dst, rsem, section):
        gather(own.at[which], dst.at[s], own_s.at[which], rsem.at[s], section, far)

        @pl.when(s == section)
        def _():
            pltpu.make_async_copy(own.at[which], dst.at[s, pl.ds(0, rows)], rsem.at[s]).start()

        @pl.when(s != section)
        def _():
            gather(own.at[which], dst.at[s], own_s.at[which], rsem.at[s], section, ((0, 0),))

    spread(0, h_full, agf_r, 0)
    load_og.wait()
    spread(1, g_full, agb_r, sections - 1)
    load_gains.wait()
    load_wu.wait()
    load_wd.wait()
    gain_row = gains[...]

    gain_acc[...] = jnp.zeros_like(gain_acc)

    def step_b(m):
        wait(g_full.at[m], agb_r.at[m])
        grad = g_full[m]
        gc_all[m, 0] = g_full[m, :, own_cols]
        cols_to_y(g_full, gc_all, m, gc_ss, gc_r)
        down_grad = dot(grad, wd_t[...], (1, 0))
        pg = (down_grad * slope_s[m]).astype(BF16)
        pg_all[m, 0] = pg
        pg_to_y(m)
        norm_grad = dot(pg, wu_t[...], (1, 0))
        normed = normed_s[m]

        @pl.when(jnp.logical_not(first))
        def _():
            scaled = norm_grad * gain_row
            back = scale_s[m][:, :1] * (
                scaled
                - jnp.mean(scaled, axis=-1, keepdims=True)
                - normed * jnp.mean(scaled * normed, axis=-1, keepdims=True)
            )
            send_b[m, pl.ds(0, rows)] = (back[:rows] + grad[:rows].astype(F32)).astype(BF16)
            send_b[m, pl.ds(rows, 3 * rows)] = back[rows:].astype(BF16)
            scatter(send_b.at[m], part_b.at[m], rsb_s.at[m], rsb_r.at[m], (s + 1) % 4 + s // 3)

        terms = norm_grad * normed
        total = terms[0:8]
        for at in range(8, full, 8):
            total = total + terms[at:at + 8]
        gain_acc[...] += total

    def transpose(weight, into):
        step = 256
        count = weight.shape[0] // step

        def piece(at, carry):
            part = pl.ds(pl.multiple_of(at * step, step), step)
            into[:, part] = weight[part].T
            return carry

        lax.fori_loop(0, count, piece, 0)

    @pl.when(jnp.logical_not(first))
    def _():
        transpose(wd, wd_t)
        transpose(wu, wu_t)

    def helping(start, stop, body):
        def run(m, carry):
            body(m)
            return carry

        lax.fori_loop(start, stop, run, 0)

    @pl.when(last)
    def _():
        helping(0, micro, lambda m: relay_f(0, m, 1))

    turn = s // (sections - 1)

    def step(i, carry):
        back = turn * (i % 2) + (1 - turn) * (i // micro)
        m = turn * (i // 2) + (1 - turn) * (i % micro)

        @pl.when(back == 0)
        def _():
            step_f(m)

        @pl.when(back == 1)
        def _():
            @pl.when(jnp.logical_and(first, m == 0))
            def _():
                helping(0, micro, lambda m: relay_f(0, m, 2))
                transpose(wd, wd_t)
                transpose(wu, wu_t)

            @pl.when(jnp.logical_and(s == 1, m == 0))
            def _():
                helping(0, micro, lambda m: relay_f(1, m, 3))
                helping(0, micro, lambda m: relay_b(m, 2))

            step_b(m)

        return carry

    lax.fori_loop(0, 2 * micro, step, 0)

    @pl.when(s >= 2)
    def _():
        helping(0, micro, lambda m: relay_b(m, s - 2))

    total = jnp.sum(gain_acc[...], axis=0, keepdims=True)
    lines = width // 128
    for line in range(lines):
        g1[0, line:line + 1] = total[:, line * 128:(line + 1) * 128]
    for dy in range(1, n_y):
        send(g1.at[0], g1.at[dy], g1_ss.at[0], g1_r.at[0], place(s, (y + dy) % n_y, z, core))

    dn_acc[...] = jnp.zeros_like(dn_acc)
    up_acc[...] = jnp.zeros_like(up_acc)

    def down_part(m, carry):
        if n_y > 1:
            wait(act_all.at[m, pl.ds(1, n_y - 1)], act_r.at[m])
            wait(gc_all.at[m, pl.ds(1, n_y - 1)], gc_r.at[m])
        cols = gc_all[m].reshape(n_y * full, span)
        dn_acc[...] += dot(cols, act_all[m].reshape(n_y * full, -1), (0, 0))
        return carry

    def up_half(m, half):
        cols = halves[half]
        if n_y > 1:
            wait(pg_all.at[m, pl.ds(1, n_y - 1), :, cols], pg_r.at[2 * m + half])
        left = nc_all[m].reshape(n_y * full, span)
        up_acc[:, cols] += dot(left, pg_all[m, :, :, cols].reshape(n_y * full, -1), (0, 0))

    def up_part(m, carry):
        if n_y > 1:
            wait(nc_all.at[m, pl.ds(1, n_y - 1)], nc_r.at[m])
        for half in range(2):
            up_half(m, half)
        return carry

    other = 1 - core

    def block(z_lo_at, core_at):
        return pl.ds(pl.multiple_of((z_lo_at * 2 + core_at) * share, share), share)

    def to_core(acc, buf, ssem, rsem, cols):
        for z_lo_at in range(2):
            buf[z_lo_at, :, cols] = acc[block(z_lo_at, other), cols].astype(BF16)
        send(buf.at[pl.ds(0, 2), :, cols], buf.at[pl.ds(2, 2), :, cols], ssem, rsem, place(s, y, z, other))

    def to_pair(acc, buf, rsem, ssem2, rsem2, cols):
        wait(buf.at[pl.ds(2, 2), :, cols], rsem)
        away = 1 - z_lo
        buf[4, :, cols] = (acc[block(away, core), cols] + buf[2 + away, :, cols].astype(F32)).astype(BF16)
        send(buf.at[4, :, cols], buf.at[5, :, cols], ssem2, rsem2, place(s, y, 2 * t + away, core))

    def finish(acc, buf, rsem2, cols):
        wait(buf.at[5, :, cols], rsem2)
        return acc[block(z_lo, core), cols] + buf[2 + z_lo, :, cols].astype(F32) + buf[5, :, cols].astype(F32)

    lax.fori_loop(0, micro, down_part, 0)
    to_core(dn_acc, dn_buf, dn_ss.at[0], dn_r.at[0], whole)

    lax.fori_loop(0, micro - 1, up_part, 0)
    to_pair(dn_acc, dn_buf, dn_r.at[0], dn2_ss.at[0], dn2_r.at[0], whole)

    if n_y > 1:
        wait(g1.at[pl.ds(1, n_y - 1)], g1_r.at[0])
    total = g1[0]
    for dy in range(1, n_y):
        total = total + g1[dy]
    g2[0] = total
    for dz in range(RING):
        for dc in range(2):
            if dz or dc:
                send(
                    g2.at[0], g2.at[dz * 2 + dc], g2_ss.at[0], g2_r.at[0],
                    place(s, y, z + dz, (core + dc) % 2),
                )

    if n_y > 1:
        wait(nc_all.at[micro - 1, pl.ds(1, n_y - 1)], nc_r.at[micro - 1])
    for half, cols in enumerate(halves):
        up_half(micro - 1, half)
        to_core(up_acc, up_buf, up_ss.at[half], up_r.at[half], cols)
        to_pair(up_acc, up_buf, up_r.at[half], up2_ss.at[half], up2_r.at[half], cols)
    dn_o[0] = finish(dn_acc, dn_buf, dn2_r.at[0], whole)

    wait(g2.at[pl.ds(1, 2 * RING - 1)], g2_r.at[0])
    total = g2[0]
    for peer in range(1, 2 * RING):
        total = total + g2[peer]
    per = gain_o.shape[1]
    fold = 128 // per
    index = p * 4 + t
    line_at = lax.broadcasted_iota(jnp.int32, total.shape, 0)
    line = jnp.sum(jnp.where(line_at == index // fold, total, 0.0), axis=0, keepdims=True)
    piece = jnp.zeros((1, per), F32)
    for at in range(fold):
        piece = piece + jnp.where(index % fold == at, line[:, at * per:(at + 1) * per], 0.0)
    gain_o[...] = piece

    for half, cols in enumerate(halves):
        up_o[0, :, cols] = finish(up_acc, up_buf, up2_r.at[half], cols)

    def drain(m, carry):
        @pl.when(jnp.logical_or(first, last))
        def _():
            wait(h_full.at[m], agf_s.at[m])

        @pl.when(s == 1)
        def _():
            wait(h_full.at[m], agf_s.at[micro + m])

        @pl.when(jnp.logical_not(last))
        def _():
            @pl.when(m == micro - 1)
            def _():
                wait(h_full.at[m], rsf_s.at[m])

        @pl.when(jnp.logical_not(first))
        def _():
            wait(g_full.at[m], agb_s.at[m])
            wait(g_full.at[m], rsb_s.at[m])

        if n_y > 1:
            wait(act_all.at[m, pl.ds(1, n_y - 1)], act_ss.at[m])
            wait(pg_all.at[m, pl.ds(1, n_y - 1)], pg_ss.at[m])
            wait(nc_all.at[m, pl.ds(1, n_y - 1)], nc_ss.at[m])
            wait(gc_all.at[m, pl.ds(1, n_y - 1)], gc_ss.at[m])
        return carry

    lax.fori_loop(0, micro, drain, 0)
    for which, section in ((0, 0), (1, sections - 1)):
        wait(h_full.at[0, pl.ds(0, 3 * rows)], own_s.at[which])

        @pl.when(s != section)
        def _():
            wait(h_full.at[0, pl.ds(0, rows)], own_s.at[which])

    if n_y > 1:
        wait(g1.at[pl.ds(1, n_y - 1)], g1_ss.at[0])
    wait(g2.at[pl.ds(1, 2 * RING - 1)], g2_ss.at[0])
    wait(dn_buf.at[pl.ds(0, 2)], dn_ss.at[0])
    for half, cols in enumerate(halves):
        wait(up_buf.at[pl.ds(0, 2), :, cols], up_ss.at[half])
        wait(up_buf.at[4, :, cols], up2_ss.at[half])
    wait(dn_buf.at[4], dn2_ss.at[0])


def settle(up, down, gain, up_o, down_o, gain_o):
    up_o[...] = up[...]
    down_o[...] = down[...]
    gain_o[...] = gain[...]


def solution(mesh):
    sections, n_dp, n_tensor = (mesh.shape[axis] for axis in ("section", "dp", "tensor"))
    n_y = n_dp // 4

    def per_device(inputs, gains, w_up, w_down, out_grad):
        micro, rows, width = inputs.shape
        hid = w_up.shape[2]
        full = 4 * rows
        span = width // n_y
        share = span // 4
        per = width // (n_dp * n_tensor)
        hbm = pl.BlockSpec(memory_space=pltpu.HBM)
        vmem = pl.BlockSpec(memory_space=pltpu.VMEM)
        dma = pltpu.SemaphoreType.DMA
        many, one = dma((micro,)), dma((1,))
        up, down, gain = pl.pallas_call(
            functools.partial(kernel, sections=sections, n_y=n_y),
            out_shape=(
                jax.ShapeDtypeStruct((1, share, hid), F32),
                jax.ShapeDtypeStruct((1, share, hid), F32),
                jax.ShapeDtypeStruct((1, per), F32),
            ),
            in_specs=[hbm] * 5,
            out_specs=(vmem, vmem, vmem),
            scratch_shapes=[
                pltpu.VMEM((width, hid), BF16),
                pltpu.VMEM((hid, width), BF16),
                pltpu.VMEM((2, rows, width), BF16),
                pltpu.VMEM((micro, full, width), BF16),
                pltpu.VMEM((2 * micro, 4, rows, width), BF16),
                pltpu.VMEM((2 * micro, rows, width), BF16),
                pltpu.VMEM((micro, full, width), BF16),
                pltpu.VMEM((micro, full, width), BF16),
                pltpu.VMEM((micro, 4, rows, width), BF16),
                pltpu.VMEM((micro, rows, width), BF16),
                pltpu.VMEM((micro, full, width), BF16),
                pltpu.VMEM((1, width), F32),
                pltpu.VMEM((micro, full, width), F32),
                pltpu.VMEM((micro, full, 128), F32),
                pltpu.VMEM((micro, full, width), BF16),
                pltpu.VMEM((micro, full, hid), F32),
                pltpu.VMEM((micro, n_y, full, hid), BF16),
                pltpu.VMEM((micro, n_y, full, hid), BF16),
                pltpu.VMEM((micro, n_y, full, span), BF16),
                pltpu.VMEM((micro, n_y, full, span), BF16),
                pltpu.VMEM((hid, width), BF16),
                pltpu.VMEM((width, hid), BF16),
                pltpu.VMEM((span, hid), F32),
                pltpu.VMEM((span, hid), F32),
                pltpu.VMEM((6, share, hid), BF16),
                pltpu.VMEM((6, share, hid), BF16),
                pltpu.VMEM((8, width), F32),
                pltpu.VMEM((n_y, width // 128, 128), F32),
                pltpu.VMEM((2 * RING, width // 128, 128), F32),
                dma((5,)),
                dma((2,)), dma((2 * micro,)), many, many, dma((2 * micro,)),
            ] + [many] * 9 + [dma((2 * micro,))] + [many] * 2 + [dma((2,))] * 12,
            compiler_params=pltpu.CompilerParams(
                collective_id=0, has_side_effects=True, vmem_limit_bytes=63 * 1024 * 1024
            ),
        )(inputs, gains, w_up, w_down, out_grad)
        up, down, gain = pl.pallas_call(
            settle,
            out_shape=tuple(jax.ShapeDtypeStruct(part.shape, F32) for part in (up, down, gain)),
            in_specs=[vmem] * 3,
            out_specs=(vmem,) * 3,
        )(up, down, gain)
        return up, jnp.swapaxes(down, 1, 2), gain

    return jax.shard_map(
        per_device,
        mesh=mesh,
        in_specs=(
            P(None, ("dp", "tensor"), None),
            P("section", None),
            P("section", None, "tensor"),
            P("section", "tensor", None),
            P(None, ("dp", "tensor"), None),
        ),
        out_specs=(
            P("section", "dp", "tensor"),
            P("section", "tensor", "dp"),
            P("section", ("dp", "tensor")),
        ),
        check_vma=False,
    )
```

```python
import functools
import math

import jax
import jax.numpy as jnp
from jax import lax
from jax.experimental import pallas as pl
from jax.experimental.pallas import tpu as pltpu
from jax.sharding import PartitionSpec as P

MESH = pl.DeviceIdType.MESH
BF16 = jnp.bfloat16
F32 = jnp.float32
EPS = 1e-05
COEF = 0.044715
ROOT = math.sqrt(2.0 / math.pi)
RING = 8


def dot(left, right, dims):
    return lax.dot_general(left, right, ((dims[:1], dims[1:]), ((), ())), preferred_element_type=F32)


def stats(rows):
    centre = rows - jnp.mean(rows, axis=-1, keepdims=True)
    spread = jnp.mean(centre * centre, axis=-1, keepdims=True)
    scale = lax.rsqrt(spread + EPS)
    return centre * scale, scale


def kernel(
    inp, gains_h, wu_h, wd_h, og,
    up_o, dn_o, gain_o,
    wu, wd, own, h_full, part_f, sum_f, send_f, g_full, part_b, sum_b, send_b,
    gains, normed_s, scale_s, norm_s, slope_s, act_all, pg_all, nc_all, gc_all,
    wu_t, wd_t, up_acc, dn_acc, up_buf, dn_buf,
    gain_acc, g1, g2,
    loc, own_s, agf_s, agf_r, rsf_s, rsf_r, agb_s, agb_r, rsb_s, rsb_r,
    act_ss, act_r, nc_ss, nc_r, pg_ss, pg_r, gc_ss, gc_r,
    up_ss, up_r, dn_ss, dn_r, up2_ss, up2_r, dn2_ss, dn2_r, g1_ss, g1_r, g2_ss, g2_r,
    *, sections, n_y,
):
    micro, rows, width = inp.shape
    full = 4 * rows
    span = width // n_y
    share = span // 4
    s = lax.axis_index("section")
    p = lax.axis_index("dp")
    t = lax.axis_index("tensor")
    core = p % 2
    z_lo = (p // 2) % 2
    y = p // 4
    z = 2 * t + z_lo
    e = 2 * z_lo - 1

    def place(section, y_at, z_at, core_at):
        z_at = (z_at + 2 * RING) % RING
        return (section, (y_at * 2 + z_at % 2) * 2 + core_at, z_at // 2)

    def send(src, dst, ssem, rsem, device):
        pltpu.make_async_remote_copy(
            src_ref=src, dst_ref=dst, send_sem=ssem, recv_sem=rsem,
            device_id=device, device_id_type=MESH,
        ).start()

    def wait(region, sem):
        pltpu.make_async_copy(region, region, sem).wait()

    load_wu = pltpu.make_async_copy(wu_h.at[0], wu, loc.at[0])
    load_wd = pltpu.make_async_copy(wd_h.at[0], wd, loc.at[1])
    first = s == 0
    last = s == sections - 1

    load_in = pltpu.make_async_copy(inp.at[s], own.at[0], loc.at[2])
    load_og = pltpu.make_async_copy(og.at[s], own.at[1], loc.at[3])
    load_in.start()
    load_og.start()
    load_gains = pltpu.make_async_copy(gains_h, gains, loc.at[4])
    load_gains.start()
    load_wu.start()
    load_wd.start()

    barrier = pltpu.get_barrier_semaphore()

    def greet(device):
        pl.semaphore_signal(barrier, inc=1, device_id=device, device_id_type=MESH)

    for dz in range(RING):
        for dc in range(2):
            if dz or dc:
                greet(place(s, y, z + dz, (core + dc) % 2))
    for dy in range(1, n_y):
        greet(place(s, (y + dy) % n_y, z, core))
    for ds in range(1, sections):
        for step in (-2, 0, 1, 2, 3):
            greet(place((s + ds) % sections, y, z + e * step, core))
    pl.semaphore_wait(barrier, 2 * RING - 1 + n_y - 1 + 5 * (sections - 1))

    def gather(src, dst, ssem, rsem, section, slots=((3, 3), (2, -2), (1, 1), (0, 0))):
        for slot, step in slots:
            send(src, dst.at[pl.ds(slot * rows, rows)], ssem, rsem, place(section, y, z + e * step, core))

    def scatter(src, dst, ssem, rsem, section):
        for slot in (3, 2, 1, 0):
            send(src.at[pl.ds(slot * rows, rows)], dst.at[slot], ssem, rsem, place(section, y, z + e * slot, core))

    def relay(part, total_ref, part_r, ssem, dst, rsem, section):
        wait(part, part_r)
        total = part[0].astype(F32)
        for slot in range(1, 4):
            total = total + part[slot].astype(F32)
        total_ref[...] = total.astype(BF16)
        gather(total_ref, dst, ssem, rsem, section)

    def relay_f(duty, m, section):
        at = duty * micro + m
        relay(part_f.at[at], sum_f.at[at], rsf_r.at[at], agf_s.at[at], h_full.at[m], agf_r.at[m], section)

    def relay_b(m, section):
        relay(part_b.at[m], sum_b.at[m], rsb_r.at[m], agb_s.at[m], g_full.at[m], agb_r.at[m], section)

    ring_y = sorted(range(1, n_y), key=lambda dy: -min(dy, n_y - dy))

    def to_y(buf, m, ssem, rsem):
        for dy in ring_y:
            send(buf.at[m, 0], buf.at[m, dy], ssem.at[m], rsem.at[m], place(s, (y + dy) % n_y, z, core))

    hid = pg_all.shape[3]
    whole = pl.ds(0, hid)
    halves = (pl.ds(0, hid // 2), pl.ds(hid // 2, hid // 2))

    def pg_to_y(m):
        for half, cols in enumerate(halves):
            for dy in ring_y:
                send(
                    pg_all.at[m, 0, :, cols], pg_all.at[m, dy, :, cols],
                    pg_ss.at[m], pg_r.at[2 * m + half], place(s, (y + dy) % n_y, z, core),
                )

    def cols_to_y(src, buf, m, ssem, rsem):
        for dy in ring_y:
            y_at = (y + dy) % n_y
            send(
                src.at[m, :, pl.ds(pl.multiple_of(y_at * span, span), span)], buf.at[m, dy],
                ssem.at[m], rsem.at[m], place(s, y_at, z, core),
            )

    own_cols = pl.ds(pl.multiple_of(y * span, span), span)

    def step_f(m):
        wait(h_full.at[m], agf_r.at[m])
        hidden = h_full[m].astype(F32)
        normed, scale = stats(hidden)
        norm = (normed * gain_row).astype(BF16)
        preact = dot(norm, wu[...], (1, 0))
        inner = ROOT * (preact + COEF * preact * preact * preact)
        tangent = jnp.tanh(inner)
        act = (0.5 * preact * (1.0 + tangent)).astype(BF16)
        act_all[m, 0] = act

        @pl.when(jnp.logical_not(last))
        def _():
            mixed = dot(act, wd[...], (1, 0))
            send_f[m, pl.ds(0, rows)] = (mixed[:rows] + hidden[:rows]).astype(BF16)
            send_f[m, pl.ds(rows, 3 * rows)] = mixed[rows:].astype(BF16)
            at = s // 2 * micro + m

            @pl.when(m > 0)
            def _():
                wait(h_full.at[m - 1], rsf_s.at[m - 1])

            scatter(send_f.at[m], part_f.at[at], rsf_s.at[m], rsf_r.at[at], (s + 3) % 4)

        slope_s[m] = 0.5 * (1.0 + tangent) + 0.5 * preact * (1.0 - tangent * tangent) * ROOT * (
            1.0 + 3.0 * COEF * preact * preact
        )
        normed_s[m] = normed
        scale_s[m] = jnp.broadcast_to(scale, (full, 128))
        norm_s[m] = norm
        nc_all[m, 0] = norm_s[m, :, own_cols]
        cols_to_y(norm_s, nc_all, m, nc_ss, nc_r)
        to_y(act_all, m, act_ss, act_r)

    load_in.wait()
    far = ((3, 3), (2, -2), (1, 1))

    def spread(which, dst, rsem, section):
        gather(own.at[which], dst.at[s], own_s.at[which], rsem.at[s], section, far)

        @pl.when(s == section)
        def _():
            pltpu.make_async_copy(own.at[which], dst.at[s, pl.ds(0, rows)], rsem.at[s]).start()

        @pl.when(s != section)
        def _():
            gather(own.at[which], dst.at[s], own_s.at[which], rsem.at[s], section, ((0, 0),))

    spread(0, h_full, agf_r, 0)
    load_og.wait()
    spread(1, g_full, agb_r, sections - 1)
    load_gains.wait()
    load_wu.wait()
    load_wd.wait()
    gain_row = gains[...]

    gain_acc[...] = jnp.zeros_like(gain_acc)

    def step_b(m):
        wait(g_full.at[m], agb_r.at[m])
        grad = g_full[m]
        gc_all[m, 0] = g_full[m, :, own_cols]
        cols_to_y(g_full, gc_all, m, gc_ss, gc_r)
        down_grad = dot(grad, wd_t[...], (1, 0))
        pg = (down_grad * slope_s[m]).astype(BF16)
        pg_all[m, 0] = pg
        pg_to_y(m)
        norm_grad = dot(pg, wu_t[...], (1, 0))
        normed = normed_s[m]

        @pl.when(jnp.logical_not(first))
        def _():
            scaled = norm_grad * gain_row
            back = scale_s[m][:, :1] * (
                scaled
                - jnp.mean(scaled, axis=-1, keepdims=True)
                - normed * jnp.mean(scaled * normed, axis=-1, keepdims=True)
            )
            send_b[m, pl.ds(0, rows)] = (back[:rows] + grad[:rows].astype(F32)).astype(BF16)
            send_b[m, pl.ds(rows, 3 * rows)] = back[rows:].astype(BF16)
            scatter(send_b.at[m], part_b.at[m], rsb_s.at[m], rsb_r.at[m], (s + 1) % 4 + s // 3)

        terms = norm_grad * normed
        total = terms[0:8]
        for at in range(8, full, 8):
            total = total + terms[at:at + 8]
        gain_acc[...] += total

    def transpose(weight, into):
        step = 256
        count = weight.shape[0] // step

        def piece(at, carry):
            part = pl.ds(pl.multiple_of(at * step, step), step)
            into[:, part] = weight[part].T
            return carry

        lax.fori_loop(0, count, piece, 0)

    @pl.when(jnp.logical_not(first))
    def _():
        transpose(wd, wd_t)
        transpose(wu, wu_t)

    def helping(start, stop, body):
        def run(m, carry):
            body(m)
            return carry

        lax.fori_loop(start, stop, run, 0)

    @pl.when(last)
    def _():
        helping(0, micro, lambda m: relay_f(0, m, 1))

    turn = s // (sections - 1)

    def step(i, carry):
        back = turn * (i % 2) + (1 - turn) * (i // micro)
        m = turn * (i // 2) + (1 - turn) * (i % micro)

        @pl.when(back == 0)
        def _():
            step_f(m)

        @pl.when(back == 1)
        def _():
            @pl.when(jnp.logical_and(first, m == 0))
            def _():
                helping(0, micro, lambda m: relay_f(0, m, 2))
                transpose(wd, wd_t)
                transpose(wu, wu_t)

            @pl.when(jnp.logical_and(s == 1, m == 0))
            def _():
                helping(0, micro, lambda m: relay_f(1, m, 3))
                helping(0, micro, lambda m: relay_b(m, 2))

            step_b(m)

        return carry

    lax.fori_loop(0, 2 * micro, step, 0)

    @pl.when(s >= 2)
    def _():
        helping(0, micro, lambda m: relay_b(m, s - 2))

    total = jnp.sum(gain_acc[...], axis=0, keepdims=True)
    lines = width // 128
    for line in range(lines):
        g1[0, line:line + 1] = total[:, line * 128:(line + 1) * 128]
    for dy in range(1, n_y):
        send(g1.at[0], g1.at[dy], g1_ss.at[0], g1_r.at[0], place(s, (y + dy) % n_y, z, core))

    dn_acc[...] = jnp.zeros_like(dn_acc)
    up_acc[...] = jnp.zeros_like(up_acc)

    def down_part(m, carry):
        if n_y > 1:
            wait(act_all.at[m, pl.ds(1, n_y - 1)], act_r.at[m])
            wait(gc_all.at[m, pl.ds(1, n_y - 1)], gc_r.at[m])
        cols = gc_all[m].reshape(n_y * full, span)
        dn_acc[...] += dot(cols, act_all[m].reshape(n_y * full, -1), (0, 0))
        return carry

    def up_half(m, half):
        cols = halves[half]
        if n_y > 1:
            wait(pg_all.at[m, pl.ds(1, n_y - 1), :, cols], pg_r.at[2 * m + half])
        left = nc_all[m].reshape(n_y * full, span)
        up_acc[:, cols] += dot(left, pg_all[m, :, :, cols].reshape(n_y * full, -1), (0, 0))

    def up_part(m, carry):
        if n_y > 1:
            wait(nc_all.at[m, pl.ds(1, n_y - 1)], nc_r.at[m])
        for half in range(2):
            up_half(m, half)
        return carry

    other = 1 - core

    def block(z_lo_at, core_at):
        return pl.ds(pl.multiple_of((z_lo_at * 2 + core_at) * share, share), share)

    def to_core(acc, buf, ssem, rsem, cols):
        for z_lo_at in range(2):
            buf[z_lo_at, :, cols] = acc[block(z_lo_at, other), cols].astype(BF16)
        send(buf.at[pl.ds(0, 2), :, cols], buf.at[pl.ds(2, 2), :, cols], ssem, rsem, place(s, y, z, other))

    def to_pair(acc, buf, rsem, ssem2, rsem2, cols):
        wait(buf.at[pl.ds(2, 2), :, cols], rsem)
        away = 1 - z_lo
        buf[4, :, cols] = (acc[block(away, core), cols] + buf[2 + away, :, cols].astype(F32)).astype(BF16)
        send(buf.at[4, :, cols], buf.at[5, :, cols], ssem2, rsem2, place(s, y, 2 * t + away, core))

    def finish(acc, buf, rsem2, cols):
        wait(buf.at[5, :, cols], rsem2)
        return acc[block(z_lo, core), cols] + buf[2 + z_lo, :, cols].astype(F32) + buf[5, :, cols].astype(F32)

    lax.fori_loop(0, micro, down_part, 0)
    to_core(dn_acc, dn_buf, dn_ss.at[0], dn_r.at[0], whole)

    lax.fori_loop(0, micro - 1, up_part, 0)
    to_pair(dn_acc, dn_buf, dn_r.at[0], dn2_ss.at[0], dn2_r.at[0], whole)

    if n_y > 1:
        wait(g1.at[pl.ds(1, n_y - 1)], g1_r.at[0])
    total = g1[0]
    for dy in range(1, n_y):
        total = total + g1[dy]
    g2[0] = total
    for dz in range(RING):
        for dc in range(2):
            if dz or dc:
                send(
                    g2.at[0], g2.at[dz * 2 + dc], g2_ss.at[0], g2_r.at[0],
                    place(s, y, z + dz, (core + dc) % 2),
                )

    if n_y > 1:
        wait(nc_all.at[micro - 1, pl.ds(1, n_y - 1)], nc_r.at[micro - 1])
    for half, cols in enumerate(halves):
        up_half(micro - 1, half)
        to_core(up_acc, up_buf, up_ss.at[half], up_r.at[half], cols)
        to_pair(up_acc, up_buf, up_r.at[half], up2_ss.at[half], up2_r.at[half], cols)
    dn_o[0] = finish(dn_acc, dn_buf, dn2_r.at[0], whole)

    wait(g2.at[pl.ds(1, 2 * RING - 1)], g2_r.at[0])
    total = g2[0]
    for peer in range(1, 2 * RING):
        total = total + g2[peer]
    per = gain_o.shape[1]
    fold = 128 // per
    index = p * 4 + t
    line_at = lax.broadcasted_iota(jnp.int32, total.shape, 0)
    line = jnp.sum(jnp.where(line_at == index // fold, total, 0.0), axis=0, keepdims=True)
    piece = jnp.zeros((1, per), F32)
    for at in range(fold):
        piece = piece + jnp.where(index % fold == at, line[:, at * per:(at + 1) * per], 0.0)
    gain_o[...] = piece

    for half, cols in enumerate(halves):
        up_o[0, :, cols] = finish(up_acc, up_buf, up2_r.at[half], cols)

    def drain(m, carry):
        @pl.when(jnp.logical_or(first, last))
        def _():
            wait(h_full.at[m], agf_s.at[m])

        @pl.when(s == 1)
        def _():
            wait(h_full.at[m], agf_s.at[micro + m])

        @pl.when(jnp.logical_not(last))
        def _():
            @pl.when(m == micro - 1)
            def _():
                wait(h_full.at[m], rsf_s.at[m])

        @pl.when(jnp.logical_not(first))
        def _():
            wait(g_full.at[m], agb_s.at[m])
            wait(g_full.at[m], rsb_s.at[m])

        if n_y > 1:
            wait(act_all.at[m, pl.ds(1, n_y - 1)], act_ss.at[m])
            wait(pg_all.at[m, pl.ds(1, n_y - 1)], pg_ss.at[m])
            wait(nc_all.at[m, pl.ds(1, n_y - 1)], nc_ss.at[m])
            wait(gc_all.at[m, pl.ds(1, n_y - 1)], gc_ss.at[m])
        return carry

    lax.fori_loop(0, micro, drain, 0)
    for which, section in ((0, 0), (1, sections - 1)):
        wait(h_full.at[0, pl.ds(0, 3 * rows)], own_s.at[which])

        @pl.when(s != section)
        def _():
            wait(h_full.at[0, pl.ds(0, rows)], own_s.at[which])

    if n_y > 1:
        wait(g1.at[pl.ds(1, n_y - 1)], g1_ss.at[0])
    wait(g2.at[pl.ds(1, 2 * RING - 1)], g2_ss.at[0])
    wait(dn_buf.at[pl.ds(0, 2)], dn_ss.at[0])
    for half, cols in enumerate(halves):
        wait(up_buf.at[pl.ds(0, 2), :, cols], up_ss.at[half])
        wait(up_buf.at[4, :, cols], up2_ss.at[half])
    wait(dn_buf.at[4], dn2_ss.at[0])


def settle(up, down, gain, up_o, down_o, gain_o):
    up_o[...] = up[...]
    down_o[...] = down[...]
    gain_o[...] = gain[...]


def solution(mesh):
    sections, n_dp, n_tensor = (mesh.shape[axis] for axis in ("section", "dp", "tensor"))
    n_y = n_dp // 4

    def per_device(inputs, gains, w_up, w_down, out_grad):
        micro, rows, width = inputs.shape
        hid = w_up.shape[2]
        full = 4 * rows
        span = width // n_y
        share = span // 4
        per = width // (n_dp * n_tensor)
        hbm = pl.BlockSpec(memory_space=pltpu.HBM)
        vmem = pl.BlockSpec(memory_space=pltpu.VMEM)
        dma = pltpu.SemaphoreType.DMA
        many, one = dma((micro,)), dma((1,))
        up, down, gain = pl.pallas_call(
            functools.partial(kernel, sections=sections, n_y=n_y),
            out_shape=(
                jax.ShapeDtypeStruct((1, share, hid), F32),
                jax.ShapeDtypeStruct((1, share, hid), F32),
                jax.ShapeDtypeStruct((1, per), F32),
            ),
            in_specs=[hbm] * 5,
            out_specs=(vmem, vmem, vmem),
            scratch_shapes=[
                pltpu.VMEM((width, hid), BF16),
                pltpu.VMEM((hid, width), BF16),
                pltpu.VMEM((2, rows, width), BF16),
                pltpu.VMEM((micro, full, width), BF16),
                pltpu.VMEM((2 * micro, 4, rows, width), BF16),
                pltpu.VMEM((2 * micro, rows, width), BF16),
                pltpu.VMEM((micro, full, width), BF16),
                pltpu.VMEM((micro, full, width), BF16),
                pltpu.VMEM((micro, 4, rows, width), BF16),
                pltpu.VMEM((micro, rows, width), BF16),
                pltpu.VMEM((micro, full, width), BF16),
                pltpu.VMEM((1, width), F32),
                pltpu.VMEM((micro, full, width), F32),
                pltpu.VMEM((micro, full, 128), F32),
                pltpu.VMEM((micro, full, width), BF16),
                pltpu.VMEM((micro, full, hid), F32),
                pltpu.VMEM((micro, n_y, full, hid), BF16),
                pltpu.VMEM((micro, n_y, full, hid), BF16),
                pltpu.VMEM((micro, n_y, full, span), BF16),
                pltpu.VMEM((micro, n_y, full, span), BF16),
                pltpu.VMEM((hid, width), BF16),
                pltpu.VMEM((width, hid), BF16),
                pltpu.VMEM((span, hid), F32),
                pltpu.VMEM((span, hid), F32),
                pltpu.VMEM((6, share, hid), BF16),
                pltpu.VMEM((6, share, hid), BF16),
                pltpu.VMEM((8, width), F32),
                pltpu.VMEM((n_y, width // 128, 128), F32),
                pltpu.VMEM((2 * RING, width // 128, 128), F32),
                dma((5,)),
                dma((2,)), dma((2 * micro,)), many, many, dma((2 * micro,)),
            ] + [many] * 9 + [dma((2 * micro,))] + [many] * 2 + [dma((2,))] * 12,
            compiler_params=pltpu.CompilerParams(
                collective_id=0, has_side_effects=True, vmem_limit_bytes=63 * 1024 * 1024
            ),
        )(inputs, gains, w_up, w_down, out_grad)
        piece = pl.BlockSpec((1, share // 2, hid), lambda at: (0, at, 0))
        line = pl.BlockSpec((1, per), lambda at: (0, 0))
        up, down, gain = pl.pallas_call(
            settle,
            out_shape=tuple(jax.ShapeDtypeStruct(part.shape, F32) for part in (up, down, gain)),
            grid=(2,),
            in_specs=[piece, piece, line],
            out_specs=(piece, piece, line),
        )(up, down, gain)
        return up, jnp.swapaxes(down, 1, 2), gain

    return jax.shard_map(
        per_device,
        mesh=mesh,
        in_specs=(
            P(None, ("dp", "tensor"), None),
            P("section", None),
            P("section", None, "tensor"),
            P("section", "tensor", None),
            P(None, ("dp", "tensor"), None),
        ),
        out_specs=(
            P("section", "dp", "tensor"),
            P("section", "tensor", "dp"),
            P("section", ("dp", "tensor")),
        ),
        check_vma=False,
    )
```
